32 devices in a mesh: groups: 2 (over x), seq: 16 (over z, y, core).
Axes of the slice: x: 2, y: 2, z: 4, core: 2. Of those that a mesh axis runs over, the one named last changes fastest.
Arguments:
- tower_in: bfloat16 [8, 4096, 768], P('groups', 'seq'), parts along dimension 0, may hold values from -6 to 6
- first_norm_scale: float32 [4, 768], replicated, may hold values from 0.5 to 2
- first_norm_shift: float32 [4, 768], replicated, may hold values from -0.5 to 0.5
- conv_weight: bfloat16 [4, 3, 768, 384], replicated, may hold values from -0.125 to 0.125
- mid_scale: float32 [4, 384], replicated, may hold values from 0.5 to 2
- second_norm_shift: float32 [4, 384], replicated, may hold values from -0.5 to 0.5
- point_weight: bfloat16 [4, 384, 768], replicated, may hold values from -0.3125 to 0.3125
Outputs:
- tower_out: bfloat16 [8, 4096, 768], P('groups', 'seq'), parts along dimension 0
The draws below stay inside these ranges and needn't reach their ends.
There are 2 independent parts, one for each index of `groups`. The reference program is written for one: setup_inputs(seed, part) draws one part's arguments, and reference() takes and returns one part's arrays. A program takes and returns all parts, laid end to end along the dimension named above; an argument that names none is the same for every part. Nothing has to cross between parts.
All inputs are finite; a program needn't handle non-finite values.
Results may differ from the reference program's by a relative error of at most 0.017.
Values may be sent and summed in bfloat16 or wider, within the bound.
No kernel may reach another device: no remote copies, remote signals or barrier semaphores. Data moves between devices by JAX's collectives and lax.ppermute only.
A program may use at most 64 MiB of HBM per device.

```python
import math
import jax
import jax.numpy as jnp

C = 768
FILTERS = 384
BLOCKS = 4
FIRST_DILATION = 32
TRACKS = 4
NBINS = 4096


def shard_levels(rng, shape, shards, low, high):
    gain, own = 1.0, jax.random.fold_in(rng, 6)
    for position, shards_of in shards:
        draws = jnp.exp(jax.random.uniform(jax.random.fold_in(own, position), (shards_of,), jnp.float32, low / len(shards), high / len(shards)))
        gain = gain * jnp.repeat(draws, shape[position] // shards_of).reshape([-1 if axis == position else 1 for axis in range(len(shape))])
    return gain


def gaussian(stream_key, dims, width, most, shards=(), dtype=jnp.bfloat16):
    loudness = shard_levels(stream_key, dims, shards, -0.22, 0.18) if shards else 1.0
    entries = jax.random.normal(stream_key, dims, jnp.float32) * width * loudness
    return jnp.minimum(jnp.maximum(entries, -most), most).astype(dtype)


def setup_inputs(seed: int = 0, part: int = 0) -> dict:
    key_of = jax.random.split(jax.random.key(seed), 8)
    part_keys = jax.random.split(jax.random.fold_in(key_of[7], part), 8)
    tower_in = gaussian(part_keys[0], (TRACKS, NBINS, C), 1.0, 6.0, ((1, 16),))
    first_norm_scale = jnp.clip(jnp.exp(jax.random.uniform(key_of[1], (BLOCKS, C), jnp.float32, math.log(0.5), math.log(2.0))), 0.5, 2.0)
    first_norm_shift = jnp.clip(jax.random.uniform(key_of[2], (BLOCKS, C), jnp.float32, -0.5, 0.5), -0.5, 0.5)
    conv_weight = gaussian(key_of[3], (BLOCKS, 3, C, FILTERS), (3 * C) ** -0.5, 0.125)
    mid_scale = jnp.clip(jnp.exp(jax.random.uniform(key_of[4], (BLOCKS, FILTERS), jnp.float32, math.log(0.5), math.log(2.0))), 0.5, 2.0)
    second_norm_shift = jnp.clip(jax.random.uniform(key_of[5], (BLOCKS, FILTERS), jnp.float32, -0.5, 0.5), -0.5, 0.5)
    point_weight = gaussian(key_of[6], (BLOCKS, FILTERS, C), FILTERS ** -0.5, 0.3125)
    return {"tower_in": tower_in, "first_norm_scale": first_norm_scale, "first_norm_shift": first_norm_shift, "conv_weight": conv_weight, "mid_scale": mid_scale, "second_norm_shift": second_norm_shift, "point_weight": point_weight}


def normalize(stream, scale_vector, shift_vec):
    return jnp.maximum(stream.astype(jnp.float32) * scale_vector + shift_vec, 0.0)


def reference(tower_in, first_norm_scale, first_norm_shift, conv_weight, mid_scale, second_norm_shift, point_weight):
    stream = tower_in
    tracks, bin_count, channels = stream.shape
    for block_number in range(BLOCKS):
        receptive_span = FIRST_DILATION * 2 ** block_number
        normed = normalize(stream, first_norm_scale[block_number], first_norm_shift[block_number]).astype(jnp.bfloat16)
        padded = jnp.pad(normed, ((0, 0), (receptive_span, receptive_span), (0, 0)))
        summed = jnp.zeros((tracks * bin_count, FILTERS), jnp.float32)
        for kernel_tap_index in range(3):
            window = padded[:, kernel_tap_index * receptive_span:kernel_tap_index * receptive_span + bin_count, :]
            window = window.reshape(tracks * bin_count, channels)
            summed = summed + jnp.dot(window, conv_weight[block_number, kernel_tap_index], preferred_element_type=jnp.float32)
        middle = jnp.maximum(summed * mid_scale[block_number] + second_norm_shift[block_number], 0.0).astype(jnp.bfloat16)
        update = jnp.dot(middle, point_weight[block_number], preferred_element_type=jnp.float32)
        flat = stream.reshape(tracks * bin_count, channels).astype(jnp.float32)
        stream = (flat + update).astype(jnp.bfloat16).reshape(tracks, bin_count, channels)
    return stream
```

```python
import functools

import jax
import jax.numpy as jnp
from jax import lax
from jax.experimental import pallas as pl
from jax.experimental.pallas import tpu as pltpu
from jax.sharding import PartitionSpec as P

FIRST_DILATION = 32
CHUNKS = 2
VMEM_LIMIT = 48 * 1024 * 1024


def finish(stream, conv, scale, shift, point):
    middle = jnp.maximum(conv * scale + shift, 0.0).astype(jnp.bfloat16)
    update = jnp.dot(middle, point, preferred_element_type=jnp.float32)
    return (stream.astype(jnp.float32) + update).astype(jnp.bfloat16)


def begin(stream, scale, shift, weight, span, even, t, local_ref, intra_ref, inter_ref):
    rows = stream.shape[0]
    normed = jnp.maximum(stream.astype(jnp.float32) * scale + shift, 0.0).astype(jnp.bfloat16)
    behind, here, ahead = (
        jnp.dot(normed, weight[0, k], preferred_element_type=jnp.float32) for k in range(3)
    )
    to_next = behind[rows - span :].astype(jnp.bfloat16)
    to_last = ahead[:span].astype(jnp.bfloat16)

    @pl.when(even)
    def _():
        intra_ref[t] = to_next
        inter_ref[t] = to_last

    @pl.when(jnp.logical_not(even))
    def _():
        intra_ref[t] = to_last
        inter_ref[t] = to_next

    if span == rows:
        local_ref[t] = here
    else:
        zeros = jnp.zeros((span, here.shape[1]), jnp.float32)
        low = jnp.concatenate([zeros, behind[: rows - span]], axis=0)
        high = jnp.concatenate([ahead[span:], zeros], axis=0)
        local_ref[t] = here + low + high


def with_halo(local_ref, intra_ref, inter_ref, even, t, span):
    local = local_ref[t]
    rows = local.shape[0]
    intra = intra_ref[t].astype(jnp.float32)
    inter = inter_ref[t].astype(jnp.float32)
    head = jnp.where(even, inter, intra)
    tail = jnp.where(even, intra, inter)
    if span == rows:
        return local + head + tail
    zeros = jnp.zeros((rows - span, local.shape[1]), jnp.float32)
    return local + jnp.concatenate([head, zeros], axis=0) + jnp.concatenate([zeros, tail], axis=0)


def first_kernel(span, stream_ref, scale_ref, shift_ref, weight_ref, local_ref, intra_ref, inter_ref):
    even = lax.rem(lax.axis_index("seq"), 2) == 0
    for t in range(stream_ref.shape[0]):
        begin(
            stream_ref[t], scale_ref[...], shift_ref[...], weight_ref, span, even, t,
            local_ref, intra_ref, inter_ref,
        )


def middle_kernel(
    span, next_span,
    stream_ref, local_ref, intra_ref, inter_ref, mid_scale_ref, mid_shift_ref, point_ref,
    scale_ref, shift_ref, weight_ref,
    out_ref, next_local_ref, next_intra_ref, next_inter_ref,
):
    even = lax.rem(lax.axis_index("seq"), 2) == 0
    for t in range(stream_ref.shape[0]):
        conv = with_halo(local_ref, intra_ref, inter_ref, even, t, span)
        stream = finish(stream_ref[t], conv, mid_scale_ref[...], mid_shift_ref[...], point_ref[0])
        out_ref[t] = stream
        begin(
            stream, scale_ref[...], shift_ref[...], weight_ref, next_span, even, t,
            next_local_ref, next_intra_ref, next_inter_ref,
        )


def last_kernel(
    span, stream_ref, local_ref, intra_ref, inter_ref, mid_scale_ref, mid_shift_ref, point_ref, out_ref
):
    even = lax.rem(lax.axis_index("seq"), 2) == 0
    for t in range(stream_ref.shape[0]):
        conv = with_halo(local_ref, intra_ref, inter_ref, even, t, span)
        out_ref[t] = finish(stream_ref[t], conv, mid_scale_ref[...], mid_shift_ref[...], point_ref[0])


def whole(shape):
    return pl.BlockSpec(shape, lambda t: (0,) * len(shape))


def pick(shape, index):
    return pl.BlockSpec(shape, lambda t: (index,) + (0,) * (len(shape) - 1))


def track(shape, base=0):
    return pl.BlockSpec((1,) + shape, lambda t: (base + t,) + (0,) * len(shape))


def local(
    tower_in, first_norm_scale, first_norm_shift, conv_weight, mid_scale, second_norm_shift, point_weight
):
    tracks, rows, channels = tower_in.shape
    blocks, _, _, filters = conv_weight.shape
    devices = lax.axis_size("seq")
    intra_pairs = [(i, i + 1) for i in range(0, devices - 1, 2)]
    inter_pairs = [(i, i + 1) for i in range(1, devices - 1, 2)]
    intra_pairs += [(b, a) for a, b in intra_pairs]
    inter_pairs += [(b, a) for a, b in inter_pairs]
    spans = [FIRST_DILATION * 2**b for b in range(blocks)]
    size = tracks // CHUNKS
    scales = [first_norm_scale[b : b + 1] for b in range(blocks)]
    shifts = [first_norm_shift[b : b + 1] for b in range(blocks)]
    mids = [mid_scale[b : b + 1] for b in range(blocks)]
    mid_shifts = [second_norm_shift[b : b + 1] for b in range(blocks)]
    params = pltpu.CompilerParams(vmem_limit_bytes=VMEM_LIMIT)

    stream_spec = track((rows, channels))
    local_spec = track((rows, filters))
    channel_spec = whole((1, channels))
    filter_spec = whole((1, filters))
    stream_shape = jax.ShapeDtypeStruct((size, rows, channels), jnp.bfloat16)
    local_shape = jax.ShapeDtypeStruct((size, rows, filters), jnp.float32)

    def halo_spec(b):
        return track((spans[b], filters))

    def halo_shape(b):
        return jax.ShapeDtypeStruct((size, spans[b], filters), jnp.bfloat16)

    def weight_spec(b):
        return pick((1, 3, channels, filters), b)

    def point_spec(b):
        return pick((1, filters, channels), b)

    conv_flops = size * rows * channels * filters * 6
    point_flops = size * rows * channels * filters * 2

    def cost(flops):
        return pl.CostEstimate(flops=2 * flops, bytes_accessed=flops // 1000, transcendentals=0)

    streams, held = [], []
    for c in range(CHUNKS):
        streams.append(lax.slice_in_dim(tower_in, c * size, (c + 1) * size, axis=0))
    for c in range(CHUNKS):
        local_sum, intra, inter = pl.pallas_call(
            functools.partial(first_kernel, spans[0]),
            grid=(size,),
            in_specs=[
                track((rows, channels), c * size), channel_spec, channel_spec, weight_spec(0)
            ],
            out_specs=[local_spec, halo_spec(0), halo_spec(0)],
            out_shape=[local_shape, halo_shape(0), halo_shape(0)],
            compiler_params=params,
            cost_estimate=cost(conv_flops),
        )(tower_in, scales[0], shifts[0], conv_weight)
        inter = lax.ppermute(inter, "seq", inter_pairs)
        intra = lax.ppermute(intra, "seq", intra_pairs)
        held.append((local_sum, intra, inter))
    for b in range(1, blocks):
        for c in range(CHUNKS):
            first = b == 1
            stream, local_sum, intra, inter = pl.pallas_call(
                functools.partial(middle_kernel, spans[b - 1], spans[b]),
                grid=(size,),
                in_specs=[
                    track((rows, channels), c * size if first else 0),
                    local_spec, halo_spec(b - 1), halo_spec(b - 1), filter_spec, filter_spec,
                    point_spec(b - 1), channel_spec, channel_spec, weight_spec(b),
                ],
                out_specs=[stream_spec, local_spec, halo_spec(b), halo_spec(b)],
                out_shape=[stream_shape, local_shape, halo_shape(b), halo_shape(b)],
                compiler_params=params,
                cost_estimate=cost(conv_flops + point_flops),
            )(
                tower_in if first else streams[c],
                *held[c], mids[b - 1], mid_shifts[b - 1], point_weight,
                scales[b], shifts[b], conv_weight,
            )
            inter = lax.ppermute(inter, "seq", inter_pairs)
            intra = lax.ppermute(intra, "seq", intra_pairs)
            streams[c] = stream
            held[c] = (local_sum, intra, inter)
    out = None
    b = blocks - 1
    outs = []
    for c in range(CHUNKS):
        outs.append(
            pl.pallas_call(
                functools.partial(last_kernel, spans[b]),
                grid=(size,),
                in_specs=[
                    stream_spec, local_spec, halo_spec(b), halo_spec(b), filter_spec, filter_spec,
                    point_spec(b),
                ],
                out_specs=stream_spec,
                out_shape=stream_shape,
                compiler_params=params,
                cost_estimate=cost(point_flops),
            )(streams[c], *held[c], mids[b], mid_shifts[b], point_weight)
        )
    return jnp.concatenate(outs, axis=0)


def solution(mesh):
    placed = (P("groups", "seq", None), P(), P(), P(), P(), P(), P())
    return jax.shard_map(
        local, mesh=mesh, in_specs=placed, out_specs=P("groups", "seq", None), check_vma=False
    )
```

```python
import functools

import jax
import jax.numpy as jnp
from jax import lax
from jax.experimental import pallas as pl
from jax.experimental.pallas import tpu as pltpu
from jax.sharding import PartitionSpec as P

FIRST_DILATION = 32
CHUNKS = 2
VMEM_LIMIT = 48 * 1024 * 1024


def finish(stream, conv, scale, shift, point):
    middle = jnp.maximum(conv * scale + shift, 0.0).astype(jnp.bfloat16)
    update = jnp.dot(middle, point, preferred_element_type=jnp.float32)
    return (stream.astype(jnp.float32) + update).astype(jnp.bfloat16)


def begin(stream, scale, shift, weight, span, even, t, local_ref, intra_ref, inter_ref):
    rows = stream.shape[0]
    normed = jnp.maximum(stream.astype(jnp.float32) * scale + shift, 0.0).astype(jnp.bfloat16)
    behind, here, ahead = (
        jnp.dot(normed, weight[0, k], preferred_element_type=jnp.float32) for k in range(3)
    )
    to_next = behind[rows - span :].astype(jnp.bfloat16)
    to_last = ahead[:span].astype(jnp.bfloat16)

    @pl.when(even)
    def _():
        intra_ref[t] = to_next
        inter_ref[t] = to_last

    @pl.when(jnp.logical_not(even))
    def _():
        intra_ref[t] = to_last
        inter_ref[t] = to_next

    if span == rows:
        local_ref[t] = here
    else:
        zeros = jnp.zeros((span, here.shape[1]), jnp.float32)
        low = jnp.concatenate([zeros, behind[: rows - span]], axis=0)
        high = jnp.concatenate([ahead[span:], zeros], axis=0)
        local_ref[t] = here + low + high


def with_halo(local_ref, intra_ref, inter_ref, even, edge, t, span):
    local = local_ref[t]
    rows = local.shape[0]
    intra = intra_ref[t].astype(jnp.float32)
    inter = jnp.where(edge, 0.0, inter_ref[t].astype(jnp.float32))
    head = jnp.where(even, inter, intra)
    tail = jnp.where(even, intra, inter)
    if span == rows:
        return local + head + tail
    zeros = jnp.zeros((rows - span, local.shape[1]), jnp.float32)
    return local + jnp.concatenate([head, zeros], axis=0) + jnp.concatenate([zeros, tail], axis=0)


def first_kernel(span, stream_ref, scale_ref, shift_ref, weight_ref, local_ref, intra_ref, inter_ref):
    even, edge = place()
    for t in range(stream_ref.shape[0]):
        begin(
            stream_ref[t], scale_ref[...], shift_ref[...], weight_ref, span, even, t,
            local_ref, intra_ref, inter_ref,
        )


def middle_kernel(
    span, next_span,
    stream_ref, local_ref, intra_ref, inter_ref, mid_scale_ref, mid_shift_ref, point_ref,
    scale_ref, shift_ref, weight_ref,
    out_ref, next_local_ref, next_intra_ref, next_inter_ref,
):
    even, edge = place()
    for t in range(stream_ref.shape[0]):
        conv = with_halo(local_ref, intra_ref, inter_ref, even, edge, t, span)
        stream = finish(stream_ref[t], conv, mid_scale_ref[...], mid_shift_ref[...], point_ref[0])
        out_ref[t] = stream
        begin(
            stream, scale_ref[...], shift_ref[...], weight_ref, next_span, even, t,
            next_local_ref, next_intra_ref, next_inter_ref,
        )


def last_kernel(
    span, stream_ref, local_ref, intra_ref, inter_ref, mid_scale_ref, mid_shift_ref, point_ref, out_ref
):
    even, edge = place()
    for t in range(stream_ref.shape[0]):
        conv = with_halo(local_ref, intra_ref, inter_ref, even, edge, t, span)
        out_ref[t] = finish(stream_ref[t], conv, mid_scale_ref[...], mid_shift_ref[...], point_ref[0])


def whole(shape):
    return pl.BlockSpec(shape, lambda t: (0,) * len(shape))


def pick(shape, index):
    return pl.BlockSpec(shape, lambda t: (index,) + (0,) * (len(shape) - 1))


def track(shape, base=0):
    return pl.BlockSpec((1,) + shape, lambda t: (base + t,) + (0,) * len(shape))


def swaps(groups, devices):
    intra, inter = [], []
    for g in range(groups):
        base = g * devices
        intra += [(base + i, base + i + 1) for i in range(0, devices - 1, 2)]
        inter += [(base + i, base + i + 1) for i in range(1, devices - 1, 2)]
    for g in range(0, groups - 1, 2):
        for end in (0, devices - 1):
            inter.append((g * devices + end, (g + 1) * devices + end))
    return tuple(pairs + [(b, a) for a, b in pairs] for pairs in (intra, inter))


def swap(value, pairs):
    return lax.ppermute(value, ("groups", "seq"), pairs)


def place():
    index = lax.axis_index("seq")
    even = lax.rem(index, 2) == 0
    edge = jnp.logical_or(index == 0, index == lax.axis_size("seq") - 1)
    return even, edge


def local(
    tower_in, first_norm_scale, first_norm_shift, conv_weight, mid_scale, second_norm_shift, point_weight
):
    tracks, rows, channels = tower_in.shape
    blocks, _, _, filters = conv_weight.shape
    devices = lax.axis_size("seq")
    intra_pairs, inter_pairs = swaps(lax.axis_size("groups"), devices)
    spans = [FIRST_DILATION * 2**b for b in range(blocks)]
    size = tracks // CHUNKS
    scales = [first_norm_scale[b : b + 1] for b in range(blocks)]
    shifts = [first_norm_shift[b : b + 1] for b in range(blocks)]
    mids = [mid_scale[b : b + 1] for b in range(blocks)]
    mid_shifts = [second_norm_shift[b : b + 1] for b in range(blocks)]
    params = pltpu.CompilerParams(vmem_limit_bytes=VMEM_LIMIT)

    stream_spec = track((rows, channels))
    local_spec = track((rows, filters))
    channel_spec = whole((1, channels))
    filter_spec = whole((1, filters))
    stream_shape = jax.ShapeDtypeStruct((size, rows, channels), jnp.bfloat16)
    local_shape = jax.ShapeDtypeStruct((size, rows, filters), jnp.float32)

    def halo_spec(b):
        return track((spans[b], filters))

    def halo_shape(b):
        return jax.ShapeDtypeStruct((size, spans[b], filters), jnp.bfloat16)

    def weight_spec(b):
        return pick((1, 3, channels, filters), b)

    def point_spec(b):
        return pick((1, filters, channels), b)

    conv_flops = size * rows * channels * filters * 6
    point_flops = size * rows * channels * filters * 2

    def cost(flops):
        return pl.CostEstimate(flops=2 * flops, bytes_accessed=flops // 1000, transcendentals=0)

    streams, held = [], []
    for c in range(CHUNKS):
        streams.append(lax.slice_in_dim(tower_in, c * size, (c + 1) * size, axis=0))
    for c in range(CHUNKS):
        local_sum, intra, inter = pl.pallas_call(
            functools.partial(first_kernel, spans[0]),
            grid=(size,),
            in_specs=[
                track((rows, channels), c * size), channel_spec, channel_spec, weight_spec(0)
            ],
            out_specs=[local_spec, halo_spec(0), halo_spec(0)],
            out_shape=[local_shape, halo_shape(0), halo_shape(0)],
            compiler_params=params,
            cost_estimate=cost(conv_flops),
        )(tower_in, scales[0], shifts[0], conv_weight)
        inter = swap(inter, inter_pairs)
        intra = swap(intra, intra_pairs)
        held.append((local_sum, intra, inter))
    for b in range(1, blocks):
        for c in range(CHUNKS):
            first = b == 1
            stream, local_sum, intra, inter = pl.pallas_call(
                functools.partial(middle_kernel, spans[b - 1], spans[b]),
                grid=(size,),
                in_specs=[
                    track((rows, channels), c * size if first else 0),
                    local_spec, halo_spec(b - 1), halo_spec(b - 1), filter_spec, filter_spec,
                    point_spec(b - 1), channel_spec, channel_spec, weight_spec(b),
                ],
                out_specs=[stream_spec, local_spec, halo_spec(b), halo_spec(b)],
                out_shape=[stream_shape, local_shape, halo_shape(b), halo_shape(b)],
                compiler_params=params,
                cost_estimate=cost(conv_flops + point_flops),
            )(
                tower_in if first else streams[c],
                *held[c], mids[b - 1], mid_shifts[b - 1], point_weight,
                scales[b], shifts[b], conv_weight,
            )
            inter = swap(inter, inter_pairs)
            intra = swap(intra, intra_pairs)
            streams[c] = stream
            held[c] = (local_sum, intra, inter)
    out = None
    b = blocks - 1
    outs = []
    for c in range(CHUNKS):
        outs.append(
            pl.pallas_call(
                functools.partial(last_kernel, spans[b]),
                grid=(size,),
                in_specs=[
                    stream_spec, local_spec, halo_spec(b), halo_spec(b), filter_spec, filter_spec,
                    point_spec(b),
                ],
                out_specs=stream_spec,
                out_shape=stream_shape,
                compiler_params=params,
                cost_estimate=cost(point_flops),
            )(streams[c], *held[c], mids[b], mid_shifts[b], point_weight)
        )
    return jnp.concatenate(outs, axis=0)


def solution(mesh):
    placed = (P("groups", "seq", None), P(), P(), P(), P(), P(), P())
    return jax.shard_map(
        local, mesh=mesh, in_specs=placed, out_specs=P("groups", "seq", None), check_vma=False
    )
```

```python
import functools

import jax
import jax.numpy as jnp
from jax import lax
from jax.experimental import pallas as pl
from jax.experimental.pallas import tpu as pltpu
from jax.sharding import PartitionSpec as P

FIRST_DILATION = 32
CHUNKS = 2
MIB = 1024 * 1024
TAPS = 3


def place():
    index = lax.axis_index("seq")
    even = lax.rem(index, 2) == 0
    edge = jnp.logical_or(index == 0, index == lax.axis_size("seq") - 1)
    return even, edge


def both_ways(body):
    even, edge = place()
    pl.when(even)(lambda: body(True, edge))
    pl.when(jnp.logical_not(even))(lambda: body(False, edge))


def normed_of(stream, scale, shift):
    return jnp.maximum(stream.astype(jnp.float32) * scale + shift, 0.0).astype(jnp.bfloat16)


def emit(products, span, even, t, rows, local_ref, intra_ref, inter_ref):
    behind, here, ahead = products
    next_ref, last_ref = (intra_ref, inter_ref) if even else (inter_ref, intra_ref)
    next_ref[t] = behind[rows - span :].astype(jnp.bfloat16)
    last_ref[t] = ahead[:span].astype(jnp.bfloat16)
    if span == rows:
        local_ref[t] = here
        return
    inner = rows - span
    if span <= inner:
        local_ref[t, :span] = here[:span] + ahead[span : 2 * span]
        if inner > span:
            local_ref[t, span:inner] = (
                here[span:inner] + behind[: inner - span] + ahead[2 * span :]
            )
        local_ref[t, inner:] = here[inner:] + behind[inner - span : inner]
    else:
        local_ref[t, :inner] = here[:inner] + ahead[span:]
        local_ref[t, inner:span] = here[inner:span]
        local_ref[t, span:] = here[span:] + behind[:inner]


def begin(streams, block, span, even, scale_ref, shift_ref, weight_ref, outs):
    tracks, rows, channels = streams.shape
    filters = weight_ref.shape[-1]
    normed = normed_of(
        streams.reshape(tracks * rows, channels),
        scale_ref[block : block + 1],
        shift_ref[block : block + 1],
    )
    weight = jnp.concatenate([weight_ref[k] for k in range(TAPS)], axis=1)
    product = jnp.dot(normed, weight, preferred_element_type=jnp.float32)
    for t in range(tracks):
        part = product[t * rows : (t + 1) * rows]
        emit(
            [part[:, k * filters : (k + 1) * filters] for k in range(TAPS)],
            span, even, t, rows, *outs,
        )


def conv_of(local_ref, intra_ref, inter_ref, even, edge, t, span):
    local = local_ref[t]
    rows = local.shape[0]
    intra = intra_ref[t].astype(jnp.float32)
    inter = jnp.where(edge, 0.0, inter_ref[t].astype(jnp.float32))
    head, tail = (inter, intra) if even else (intra, inter)
    if span == rows:
        return local + head + tail
    if 2 * span == rows:
        return local + jnp.concatenate([head, tail], axis=0)
    return jnp.concatenate(
        [local[:span] + head, local[span : rows - span], local[rows - span :] + tail], axis=0
    )


def finish(streams, block, span, even, edge, held, scale_ref, shift_ref, point_ref):
    tracks, rows, channels = streams.shape
    conv = jnp.concatenate([conv_of(*held, even, edge, t, span) for t in range(tracks)], axis=0)
    middle = jnp.maximum(
        conv * scale_ref[block : block + 1] + shift_ref[block : block + 1], 0.0
    ).astype(jnp.bfloat16)
    update = jnp.dot(middle, point_ref[block], preferred_element_type=jnp.float32)
    flat = streams.reshape(tracks * rows, channels).astype(jnp.float32)
    return (flat + update).astype(jnp.bfloat16).reshape(tracks, rows, channels)


def taps_of(weight_ref, block, weight, sems):
    copies = [
        pltpu.make_async_copy(weight_ref.at[block, k], weight.at[k], sems.at[k])
        for k in range(TAPS)
    ]
    for copy in copies:
        copy.start()
    return copies


def entry_kernel(
    base, span, tower_ref, scale_ref, shift_ref, weight_ref,
    out_ref, local_ref, intra_ref, inter_ref, scale, shift, weight, sems,
):
    tracks, rows, channels = out_ref.shape
    first = [
        pltpu.make_async_copy(tower_ref.at[base : base + tracks], out_ref, sems.at[TAPS]),
        pltpu.make_async_copy(scale_ref, scale, sems.at[TAPS + 1]),
        pltpu.make_async_copy(shift_ref, shift, sems.at[TAPS + 2]),
    ]
    for copy in first:
        copy.start()
    taps = taps_of(weight_ref, 0, weight, sems)
    for copy in first:
        copy.wait()
    normed = normed_of(out_ref[...].reshape(tracks * rows, channels), scale[0:1], shift[0:1])
    products = []
    for k in range(TAPS):
        taps[k].wait()
        products.append(jnp.dot(normed, weight[k], preferred_element_type=jnp.float32))

    def store(even, edge):
        for t in range(tracks):
            emit(
                [p[t * rows : (t + 1) * rows] for p in products],
                span, even, t, rows, local_ref, intra_ref, inter_ref,
            )

    both_ways(store)


def middle_kernel(
    block, spans,
    stream_ref, local_ref, intra_ref, inter_ref, mid_scale_ref, mid_shift_ref, point_ref,
    scale_ref, shift_ref, weight_ref,
    out_ref, next_local_ref, next_intra_ref, next_inter_ref, weight, sems,
):
    taps = taps_of(weight_ref, block + 1, weight, sems)

    def body(even, edge):
        stream = finish(
            stream_ref[...], block, spans[block], even, edge,
            (local_ref, intra_ref, inter_ref), mid_scale_ref, mid_shift_ref, point_ref,
        )
        out_ref[...] = stream
        for copy in taps:
            copy.wait()
        begin(
            stream, block + 1, spans[block + 1], even, scale_ref, shift_ref, weight,
            (next_local_ref, next_intra_ref, next_inter_ref),
        )

    both_ways(body)


def last_kernel(
    base, block, span,
    stream_ref, local_ref, intra_ref, inter_ref, mid_scale_ref, mid_shift_ref, point_ref, *rest
):
    out_ref, result, sem = rest[-3:]
    tracks = local_ref.shape[0]

    def body(even, edge):
        result[...] = finish(
            stream_ref[...], block, span, even, edge,
            (local_ref, intra_ref, inter_ref), mid_scale_ref, mid_shift_ref, point_ref,
        )

    both_ways(body)
    copy = pltpu.make_async_copy(result, out_ref.at[base : base + tracks], sem)
    copy.start()
    copy.wait()


def swaps(groups, devices):
    intra, inter = [], []
    for g in range(groups):
        base = g * devices
        intra += [(base + i, base + i + 1) for i in range(0, devices - 1, 2)]
        inter += [(base + i, base + i + 1) for i in range(1, devices - 1, 2)]
    for g in range(0, groups - 1, 2):
        for end in (0, devices - 1):
            inter.append((g * devices + end, (g + 1) * devices + end))
    return tuple(pairs + [(b, a) for a, b in pairs] for pairs in (intra, inter))


def swap(value, pairs):
    return lax.ppermute(value, ("groups", "seq"), pairs)


def local(
    tower_in, first_norm_scale, first_norm_shift, conv_weight, mid_scale, second_norm_shift, point_weight
):
    tracks, rows, channels = tower_in.shape
    blocks, _, _, filters = conv_weight.shape
    intra_pairs, inter_pairs = swaps(lax.axis_size("groups"), lax.axis_size("seq"))
    spans = [FIRST_DILATION * 2**b for b in range(blocks)]
    size = tracks // CHUNKS
    vmem = pl.BlockSpec(memory_space=pltpu.VMEM)
    hbm = pl.BlockSpec(memory_space=pltpu.HBM)

    def params(limit=24):
        return pltpu.CompilerParams(vmem_limit_bytes=limit * MIB)

    stream_shape = jax.ShapeDtypeStruct((size, rows, channels), jnp.bfloat16)
    conv_flops = size * rows * channels * filters * 6
    point_flops = size * rows * channels * filters * 2

    def emitted(b):
        halo = jax.ShapeDtypeStruct((size, spans[b], filters), jnp.bfloat16)
        return [jax.ShapeDtypeStruct((size, rows, filters), jnp.float32), halo, halo]

    def cost(flops):
        return pl.CostEstimate(flops=flops, bytes_accessed=flops // 1000, transcendentals=0)

    def exchange(local_sum, intra, inter):
        inter = swap(inter, inter_pairs)
        intra = swap(intra, intra_pairs)
        return local_sum, intra, inter

    far = [
        pltpu.with_memory_space_constraint(x, pltpu.HBM)
        for x in (tower_in, first_norm_scale, first_norm_shift, conv_weight)
    ]
    taps = [
        pltpu.VMEM((TAPS, channels, filters), jnp.bfloat16),
        pltpu.SemaphoreType.DMA((TAPS + 3,)),
    ]
    held, streams = [None] * CHUNKS, [None] * CHUNKS
    for c in range(CHUNKS):
        streams[c], *made = pl.pallas_call(
            functools.partial(entry_kernel, c * size, spans[0]),
            in_specs=[hbm] * 4,
            out_specs=[vmem] * 4,
            out_shape=[stream_shape] + emitted(0),
            scratch_shapes=[pltpu.VMEM(first_norm_scale.shape, jnp.float32)] * 2 + taps,
            compiler_params=params(),
            cost_estimate=cost(conv_flops),
        )(*far)
        held[c] = exchange(*made)
    for b in range(1, blocks):
        for c in range(CHUNKS):
            streams[c], *made = pl.pallas_call(
                functools.partial(middle_kernel, b - 1, spans),
                in_specs=[vmem] * 9 + [hbm],
                out_specs=[vmem] * 4,
                out_shape=[stream_shape] + emitted(b),
                scratch_shapes=taps,
                compiler_params=params(),
                cost_estimate=cost(conv_flops + point_flops),
            )(
                streams[c], *held[c], mid_scale, second_norm_shift, point_weight,
                first_norm_scale, first_norm_shift, conv_weight,
            )
            held[c] = exchange(*made)
    b = blocks - 1
    out = []
    for c in range(CHUNKS):
        out = [
            pl.pallas_call(
                functools.partial(last_kernel, c * size, b, spans[b]),
                in_specs=[vmem] * 7 + [hbm] * len(out),
                out_specs=hbm,
                out_shape=jax.ShapeDtypeStruct(tower_in.shape, jnp.bfloat16),
                scratch_shapes=[
                    pltpu.VMEM((size, rows, channels), jnp.bfloat16),
                    pltpu.SemaphoreType.DMA,
                ],
                input_output_aliases={7: 0} if out else {},
                compiler_params=params(),
                cost_estimate=cost(point_flops),
            )(streams[c], *held[c], mid_scale, second_norm_shift, point_weight, *out)
        ]
    return out[0]


def solution(mesh):
    placed = (P("groups", "seq", None), P(), P(), P(), P(), P(), P())
    return jax.shard_map(
        local, mesh=mesh, in_specs=placed, out_specs=P("groups", "seq", None), check_vma=False
    )
```

```python
import functools

import jax
import jax.numpy as jnp
from jax import lax
from jax.experimental import pallas as pl
from jax.experimental.pallas import tpu as pltpu
from jax.sharding import PartitionSpec as P

FIRST_DILATION = 32
MIB = 1024 * 1024
TAPS = 3


def place():
    index = lax.axis_index("seq")
    even = lax.rem(index, 2) == 0
    edge = jnp.logical_or(index == 0, index == lax.axis_size("seq") - 1)
    return even, edge


def both_ways(body):
    even, edge = place()
    pl.when(even)(lambda: body(True, edge))
    pl.when(jnp.logical_not(even))(lambda: body(False, edge))


def span_of(q, within, even):
    if even:
        return slice(q[0] - within[0], q[1] - within[0])
    return slice(within[1] - q[1], within[1] - q[0])


def value_term(value, within, even):
    return within, lambda q: value[span_of(q, within, even)]


def ref_term(ref, t, within, even, drop=None):
    def get(q):
        part = ref[t, span_of(q, within, even)].astype(jnp.float32)
        return part if drop is None else jnp.where(drop, 0.0, part)

    return within, get


def assemble(q, terms, even):
    cuts = sorted({q[0], q[1], *(min(max(c, q[0]), q[1]) for rows, _ in terms for c in rows)})
    pieces = []
    for low, high in zip(cuts[:-1], cuts[1:]):
        total = None
        for rows, get in terms:
            if rows[0] <= low and high <= rows[1]:
                part = get((low, high))
                total = part if total is None else total + part
        pieces.append(total)
    if not even:
        pieces = pieces[::-1]
    return pieces[0] if len(pieces) == 1 else jnp.concatenate(pieces, axis=0)


def moved(value, within, q, by, even):
    return (q[0] + by, q[1] + by), lambda to: value[
        span_of((to[0] - by, to[1] - by), within, even)
    ]


def normed_of(stream, scale, shift):
    return jnp.maximum(stream.astype(jnp.float32) * scale + shift, 0.0).astype(jnp.bfloat16)


def products_of(stream, block, even, scale_ref, shift_ref, weight_ref):
    filters = weight_ref.shape[-1]
    normed = normed_of(stream, scale_ref[block : block + 1], shift_ref[block : block + 1])
    weight = jnp.concatenate([weight_ref[block, k] for k in range(TAPS)], axis=1)
    product = jnp.dot(normed, weight, preferred_element_type=jnp.float32)
    behind, here, ahead = (product[:, k * filters : (k + 1) * filters] for k in range(TAPS))
    return (ahead, here, behind) if even else (behind, here, ahead)


def finished(stream, conv, block, scale_ref, shift_ref, point_ref):
    middle = jnp.maximum(
        conv * scale_ref[block : block + 1] + shift_ref[block : block + 1], 0.0
    ).astype(jnp.bfloat16)
    update = jnp.dot(middle, point_ref[block], preferred_element_type=jnp.float32)
    return (stream.astype(jnp.float32) + update).astype(jnp.bfloat16)


def stacked(parts):
    return jnp.concatenate(parts, axis=0)


def edge_kernel(
    span, tower_ref, scale_ref, shift_ref, weight_ref, intra_ref, inter_ref,
    low, high, scale, shift, weight, sems,
):
    tracks, rows, channels = tower_ref.shape
    sources = [
        (scale_ref, scale),
        (shift_ref, shift),
        (tower_ref.at[:, 0:span], low),
        (weight_ref.at[0, TAPS - 1], weight.at[0]),
        (tower_ref.at[:, rows - span : rows], high),
        (weight_ref.at[0, 0], weight.at[1]),
    ]
    copies = [
        pltpu.make_async_copy(source, target, sems.at[i])
        for i, (source, target) in enumerate(sources)
    ]
    for copy in copies:
        copy.start()
    for copy in copies[:3]:
        copy.wait()

    def product(stream, which):
        normed = normed_of(
            stream[...].reshape(tracks * span, channels), scale[0:1], shift[0:1]
        )
        copies[3 + 2 * which].wait()
        return (
            jnp.dot(normed, weight[which], preferred_element_type=jnp.float32)
            .astype(jnp.bfloat16)
            .reshape(tracks, span, -1)
        )

    to_last = product(low, 0)
    copies[4].wait()
    to_next = product(high, 1)

    def store(even, edge):
        inter_ref[...] = to_last if even else to_next
        intra_ref[...] = to_next if even else to_last

    both_ways(store)


def entry_kernel(span, tower_ref, scale_ref, shift_ref, weight_ref, local_ref):
    tracks, rows, channels = tower_ref.shape
    everything = (0, rows)

    def body(even, edge):
        out, here, inn = products_of(
            tower_ref[...].reshape(tracks * rows, channels),
            0, even, scale_ref, shift_ref, weight_ref,
        )
        for t in range(tracks):
            own = slice(t * rows, (t + 1) * rows)
            local_ref[t] = assemble(
                everything,
                [
                    value_term(here[own], everything, even),
                    moved(out[own], everything, (span, rows), -span, even),
                    moved(inn[own], everything, (0, rows - span), span, even),
                ],
                even,
            )

    both_ways(body)


def step_kernel(plan, *refs):
    block, q, streams, terms, sends, keep = plan
    refs = list(refs)
    take = lambda n: [refs.pop(0) for _ in range(n)]
    stream_refs, term_refs = take(len(streams)), take(len(terms))
    mid_scale_ref, mid_shift_ref, point_ref = take(3)
    scale_ref, shift_ref, weight_ref = take(3)
    refs = refs[-(1 + len(sends) + len(keep)) :]
    out_ref = refs.pop(0)
    send_refs, keep_refs = take(len(sends)), take(len(keep))
    tracks, count = out_ref.shape[0], q[1] - q[0]

    def body(even, edge):
        conv = stacked(
            [
                assemble(
                    q,
                    [
                        ref_term(ref, t, rows, even, edge if crossed else None)
                        for ref, (rows, crossed) in zip(term_refs, terms)
                    ],
                    even,
                )
                for t in range(tracks)
            ]
        )
        stream = stacked(
            [
                assemble_stream(q, stream_refs, streams, t, even)
                for t in range(tracks)
            ]
        )
        stream = finished(stream, conv, block, mid_scale_ref, mid_shift_ref, point_ref)
        out_ref[...] = stream.reshape(out_ref.shape)
        named = dict(
            zip(
                ("out", "here", "inn"),
                products_of(stream, block + 1, even, scale_ref, shift_ref, weight_ref),
            )
        )
        for t in range(tracks):
            own = slice(t * count, (t + 1) * count)
            for ref, (name, rows) in zip(send_refs, sends):
                ref[t] = named[name][own][span_of(rows, q, even)].astype(jnp.bfloat16)
            for ref, (rows, parts) in zip(keep_refs, keep):
                ref[t] = assemble(
                    rows,
                    [moved(named[name][own], q, part, by, even) for name, part, by in parts],
                    even,
                )

    both_ways(body)


def assemble_stream(q, stream_refs, streams, t, even):
    pieces = []
    for ref, within in zip(stream_refs, streams):
        low, high = max(q[0], within[0]), min(q[1], within[1])
        if low < high:
            pieces.append(ref[t, span_of((low, high), within, even)])
    if not even:
        pieces = pieces[::-1]
    return pieces[0] if len(pieces) == 1 else jnp.concatenate(pieces, axis=0)


def last_kernel(block, q, rows, stream_ref, local_ref, intra_ref, inter_ref, *refs):
    mid_scale_ref, mid_shift_ref, point_ref = refs[:3]
    out_ref, result, sems = refs[-3:]
    tracks, count, channels = stream_ref.shape

    def body(even, edge):
        conv = stacked(
            [
                local_ref[t]
                + intra_ref[t].astype(jnp.float32)
                + jnp.where(edge, 0.0, inter_ref[t].astype(jnp.float32))
                for t in range(tracks)
            ]
        )
        stream = stream_ref[...].reshape(tracks * count, channels)
        target = span_of(q, (0, rows), even)
        result[...] = finished(
            stream, conv, block, mid_scale_ref, mid_shift_ref, point_ref
        ).reshape(result.shape)
        copy = pltpu.make_async_copy(result, out_ref.at[:, target], sems.at[0])
        copy.start()
        copy.wait()

    both_ways(body)


def swaps(groups, devices):
    intra, inter = [], []
    for g in range(groups):
        base = g * devices
        intra += [(base + i, base + i + 1) for i in range(0, devices - 1, 2)]
        inter += [(base + i, base + i + 1) for i in range(1, devices - 1, 2)]
    for g in range(0, groups - 1, 2):
        for end in (0, devices - 1):
            inter.append((g * devices + end, (g + 1) * devices + end))
    return tuple(pairs + [(b, a) for a, b in pairs] for pairs in (intra, inter))


def local(
    tower_in, first_norm_scale, first_norm_shift, conv_weight, mid_scale, second_norm_shift, point_weight
):
    tracks, rows, channels = tower_in.shape
    blocks, _, _, filters = conv_weight.shape
    intra_pairs, inter_pairs = swaps(lax.axis_size("groups"), lax.axis_size("seq"))
    spans = [FIRST_DILATION * 2**b for b in range(blocks)]
    vmem = pl.BlockSpec(memory_space=pltpu.VMEM)
    hbm = pl.BlockSpec(memory_space=pltpu.HBM)
    params = pltpu.CompilerParams(vmem_limit_bytes=32 * MIB)
    norms = (first_norm_scale, first_norm_shift)
    mids = (mid_scale, second_norm_shift, point_weight)

    def cross(value):
        return lax.ppermute(value, ("groups", "seq"), inter_pairs)

    def across(value):
        return lax.ppermute(value, ("groups", "seq"), intra_pairs)

    def cost(count, conv=1, point=1):
        flops = 8 * tracks * count * channels * filters * (TAPS * conv + point)
        return pl.CostEstimate(flops=flops, bytes_accessed=flops // 1000, transcendentals=0)

    def halo(count):
        return jax.ShapeDtypeStruct((tracks, count, filters), jnp.bfloat16)

    def sums(count):
        return jax.ShapeDtypeStruct((tracks, count, filters), jnp.float32)

    def step(block, q, streams, terms, sends, keep, after=()):
        plan = (
            block, q, [r for r, _ in streams], [(r, c) for r, c, _ in terms], sends, keep,
        )
        arrays = [a for _, a in streams] + [a for _, _, a in terms]
        count = q[1] - q[0]
        made = pl.pallas_call(
            functools.partial(step_kernel, plan),
            in_specs=[vmem] * (len(arrays) + 6 + len(after)),
            out_specs=[vmem] * (1 + len(sends) + len(keep)),
            out_shape=[jax.ShapeDtypeStruct((tracks, count, channels), jnp.bfloat16)]
            + [halo(r[1] - r[0]) for _, r in sends]
            + [sums(r[1] - r[0]) for r, _ in keep],
            compiler_params=params,
            cost_estimate=cost(count),
        )(*arrays, *mids, *norms, conv_weight, *after)
        return made[0], made[1 : 1 + len(sends)], made[1 + len(sends) :]

    everything = (0, rows)
    one, two, three, four = spans

    far = [
        pltpu.with_memory_space_constraint(x, pltpu.HBM)
        for x in (tower_in, first_norm_scale, first_norm_shift, conv_weight)
    ]
    intra, inter = pl.pallas_call(
        functools.partial(edge_kernel, one),
        in_specs=[hbm] * 4,
        out_specs=[vmem] * 2,
        out_shape=[halo(one)] * 2,
        scratch_shapes=[pltpu.VMEM((tracks, one, channels), jnp.bfloat16)] * 2
        + [pltpu.VMEM(first_norm_scale.shape, jnp.float32)] * 2
        + [pltpu.VMEM((2, channels, filters), jnp.bfloat16), pltpu.SemaphoreType.DMA((6,))],
        compiler_params=params,
        cost_estimate=cost(one, point=0),
    )(*far)
    inter_0, intra_0 = cross(inter), across(intra)
    local_0 = pl.pallas_call(
        functools.partial(entry_kernel, one),
        in_specs=[vmem] * 4,
        out_specs=vmem,
        out_shape=sums(rows),
        compiler_params=params,
        cost_estimate=cost(rows, point=0),
    )(tower_in, *norms, conv_weight)

    stream_1, (inter, intra), (local_1,) = step(
        0, everything,
        [(everything, tower_in)],
        [(everything, False, local_0), ((0, one), True, inter_0), ((rows - one, rows), False, intra_0)],
        [("out", (0, two)), ("inn", (rows - two, rows))],
        [
            (
                everything,
                [
                    ("here", everything, 0),
                    ("out", (two, rows), -two),
                    ("inn", (0, rows - two), two),
                ],
            )
        ],
    )
    inter_1, intra_1 = cross(inter), across(intra)

    near = (two, rows)
    stream_2n, (inter, intra), (local_2n,) = step(
        1, near,
        [(everything, stream_1)],
        [(everything, False, local_1), ((rows - two, rows), False, intra_1)],
        [("out", (two, three)), ("inn", (rows - three, rows))],
        [
            (
                everything,
                [
                    ("here", near, 0),
                    ("out", (three, rows), -three),
                    ("inn", (two, rows - three), three),
                ],
            )
        ],
    )
    inter_2n, intra_2 = cross(inter), across(intra)
    stream_2f, (inter,), (here_2f, inn_2f) = step(
        1, (0, two),
        [(everything, stream_1)],
        [(everything, False, local_1), ((0, two), True, inter_1)],
        [("out", (0, two))],
        [((0, two), [("here", (0, two), 0)]), ((three, three + two), [("inn", (0, two), three)])],
        after=(local_2n,),
    )
    inter_2f = cross(inter)

    near = (three, rows)
    streams = [((0, two), stream_2f), ((two, rows), stream_2n)]
    stream_3n, (inter, intra), (local_3n,) = step(
        2, near,
        streams[1:],
        [
            (everything, False, local_2n),
            ((three, three + two), False, inn_2f),
            ((rows - three, rows), False, intra_2),
        ],
        [("out", near), ("inn", near)],
        [(near, [("here", near, 0)])],
    )
    inter_3n, intra_3n = cross(inter), across(intra)
    stream_3f, (inter, intra), (local_3f,) = step(
        2, (0, three),
        streams,
        [
            (everything, False, local_2n),
            ((0, two), False, here_2f),
            ((0, two), True, inter_2n),
            ((two, three), True, inter_2f),
        ],
        [("out", (0, three)), ("inn", (0, three))],
        [((0, three), [("here", (0, three), 0)])],
        after=(local_3n,),
    )
    inter_3f, intra_3f = cross(inter), across(intra)

    out = []
    for q, arrays in (
        ((0, three), (stream_3f, local_3f, intra_3n, inter_3n)),
        (near, (stream_3n, local_3n, intra_3f, inter_3f)),
    ):
        count = q[1] - q[0]
        out = [
            pl.pallas_call(
                functools.partial(last_kernel, blocks - 1, q, rows),
                in_specs=[vmem] * 7 + [hbm] * len(out),
                out_specs=hbm,
                out_shape=jax.ShapeDtypeStruct(tower_in.shape, jnp.bfloat16),
                scratch_shapes=[
                    pltpu.VMEM((tracks, count, channels), jnp.bfloat16),
                    pltpu.SemaphoreType.DMA((1,)),
                ],
                input_output_aliases={7: 0} if out else {},
                compiler_params=params,
                cost_estimate=cost(count, conv=0),
            )(*arrays, *mids, *out)
        ]
    return out[0]


def solution(mesh):
    placed = (P("groups", "seq", None), P(), P(), P(), P(), P(), P())
    return jax.shard_map(
        local, mesh=mesh, in_specs=placed, out_specs=P("groups", "seq", None), check_vma=False
    )
```

```python
import functools

import jax
import jax.numpy as jnp
from jax import lax
from jax.experimental import pallas as pl
from jax.experimental.pallas import tpu as pltpu
from jax.sharding import PartitionSpec as P

FIRST_DILATION = 32
MIB = 1024 * 1024
TAPS = 3


def place():
    index = lax.axis_index("seq")
    even = lax.rem(index, 2) == 0
    edge = jnp.logical_or(index == 0, index == lax.axis_size("seq") - 1)
    return even, edge


def both_ways(body):
    even, edge = place()
    pl.when(even)(lambda: body(True, edge))
    pl.when(jnp.logical_not(even))(lambda: body(False, edge))


def span_of(q, within, even):
    if even:
        return slice(q[0] - within[0], q[1] - within[0])
    return slice(within[1] - q[1], within[1] - q[0])


def value_term(value, within, even):
    return within, lambda q: value[span_of(q, within, even)]


def ref_term(ref, t, within, even, drop=None):
    def get(q):
        part = ref[t, span_of(q, within, even)].astype(jnp.float32)
        return part if drop is None else jnp.where(drop, 0.0, part)

    return within, get


def assemble(q, terms, even):
    cuts = sorted({q[0], q[1], *(min(max(c, q[0]), q[1]) for rows, _ in terms for c in rows)})
    pieces = []
    for low, high in zip(cuts[:-1], cuts[1:]):
        total = None
        for rows, get in terms:
            if rows[0] <= low and high <= rows[1]:
                part = get((low, high))
                total = part if total is None else total + part
        pieces.append(total)
    if not even:
        pieces = pieces[::-1]
    return pieces[0] if len(pieces) == 1 else jnp.concatenate(pieces, axis=0)


def moved(value, within, q, by, even):
    return (q[0] + by, q[1] + by), lambda to: value[
        span_of((to[0] - by, to[1] - by), within, even)
    ]


def normed_of(stream, scale, shift):
    return jnp.maximum(stream.astype(jnp.float32) * scale + shift, 0.0).astype(jnp.bfloat16)


def products_of(stream, block, even, scale_ref, shift_ref, weight_ref):
    filters = weight_ref.shape[-1]
    normed = normed_of(stream, scale_ref[block : block + 1], shift_ref[block : block + 1])
    weight = jnp.concatenate([weight_ref[block, k] for k in range(TAPS)], axis=1)
    product = jnp.dot(normed, weight, preferred_element_type=jnp.float32)
    behind, here, ahead = (product[:, k * filters : (k + 1) * filters] for k in range(TAPS))
    return (ahead, here, behind) if even else (behind, here, ahead)


def finished(stream, conv, block, scale_ref, shift_ref, point_ref):
    middle = jnp.maximum(
        conv * scale_ref[block : block + 1] + shift_ref[block : block + 1], 0.0
    ).astype(jnp.bfloat16)
    update = jnp.dot(middle, point_ref[block], preferred_element_type=jnp.float32)
    return (stream.astype(jnp.float32) + update).astype(jnp.bfloat16)


def stacked(parts):
    return jnp.concatenate(parts, axis=0)


def edge_kernel(
    span, tower_ref, scale_ref, shift_ref, weight_ref, intra_ref, inter_ref,
    low, high, scale, shift, weight, sems,
):
    tracks, rows, channels = tower_ref.shape
    sources = [
        (scale_ref, scale),
        (shift_ref, shift),
        (tower_ref.at[:, 0:span], low),
        (weight_ref.at[0, TAPS - 1], weight.at[0]),
        (tower_ref.at[:, rows - span : rows], high),
        (weight_ref.at[0, 0], weight.at[1]),
    ]
    copies = [
        pltpu.make_async_copy(source, target, sems.at[i])
        for i, (source, target) in enumerate(sources)
    ]
    for copy in copies:
        copy.start()
    for copy in copies[:3]:
        copy.wait()

    def product(stream, which):
        normed = normed_of(
            stream[...].reshape(tracks * span, channels), scale[0:1], shift[0:1]
        )
        copies[3 + 2 * which].wait()
        return (
            jnp.dot(normed, weight[which], preferred_element_type=jnp.float32)
            .astype(jnp.bfloat16)
            .reshape(tracks, span, -1)
        )

    to_last = product(low, 0)
    copies[4].wait()
    to_next = product(high, 1)

    def store(even, edge):
        inter_ref[...] = to_last if even else to_next
        intra_ref[...] = to_next if even else to_last

    both_ways(store)


def entry_kernel(span, tower_ref, scale_ref, shift_ref, weight_ref, local_ref):
    tracks, rows, channels = tower_ref.shape
    everything = (0, rows)

    def body(even, edge):
        out, here, inn = products_of(
            tower_ref[...].reshape(tracks * rows, channels),
            0, even, scale_ref, shift_ref, weight_ref,
        )
        for t in range(tracks):
            own = slice(t * rows, (t + 1) * rows)
            local_ref[t] = assemble(
                everything,
                [
                    value_term(here[own], everything, even),
                    moved(out[own], everything, (span, rows), -span, even),
                    moved(inn[own], everything, (0, rows - span), span, even),
                ],
                even,
            )

    both_ways(body)


def step_kernel(plan, *refs):
    block, q, first, streams, terms, sends, keep = plan
    refs = list(refs)
    take = lambda n: [refs.pop(0) for _ in range(n)]
    stream_refs, term_refs = take(len(streams)), take(len(terms))
    mid_scale_ref, mid_shift_ref, point_ref = take(3)
    scale_ref, shift_ref, weight_ref = take(3)
    refs = refs[-(1 + len(sends) + len(keep)) :]
    out_ref = refs.pop(0)
    send_refs, keep_refs = take(len(sends)), take(len(keep))
    tracks, count = out_ref.shape[0], q[1] - q[0]

    def body(even, edge):
        conv = stacked(
            [
                assemble(
                    q,
                    [
                        ref_term(ref, first + t, rows, even, edge if crossed else None)
                        for ref, (rows, crossed) in zip(term_refs, terms)
                    ],
                    even,
                )
                for t in range(tracks)
            ]
        )
        stream = stacked(
            [
                assemble_stream(q, stream_refs, streams, first + t, even)
                for t in range(tracks)
            ]
        )
        stream = finished(stream, conv, block, mid_scale_ref, mid_shift_ref, point_ref)
        out_ref[...] = stream.reshape(out_ref.shape)
        named = dict(
            zip(
                ("out", "here", "inn"),
                products_of(stream, block + 1, even, scale_ref, shift_ref, weight_ref),
            )
        )
        for t in range(tracks):
            own = slice(t * count, (t + 1) * count)
            for ref, (name, rows) in zip(send_refs, sends):
                ref[t] = named[name][own][span_of(rows, q, even)].astype(jnp.bfloat16)
            for ref, (rows, parts) in zip(keep_refs, keep):
                ref[t] = assemble(
                    rows,
                    [moved(named[name][own], q, part, by, even) for name, part, by in parts],
                    even,
                )

    both_ways(body)


def assemble_stream(q, stream_refs, streams, t, even):
    pieces = []
    for ref, within in zip(stream_refs, streams):
        low, high = max(q[0], within[0]), min(q[1], within[1])
        if low < high:
            pieces.append(ref[t, span_of((low, high), within, even)])
    if not even:
        pieces = pieces[::-1]
    return pieces[0] if len(pieces) == 1 else jnp.concatenate(pieces, axis=0)


def last_kernel(
    block, q, rows, first, bases, stream_ref, local_ref, intra_ref, inter_ref, *refs
):
    mid_scale_ref, mid_shift_ref, point_ref = refs[:3]
    out_ref, result, sems = refs[-3:]

    def body(even, edge):
        target = span_of(q, (0, rows), even)
        copies = []
        for t in range(result.shape[0]):
            stream, local, intra, inter = (
                ref[base + t]
                for ref, base in zip((stream_ref, local_ref, intra_ref, inter_ref), bases)
            )
            conv = (
                local
                + intra.astype(jnp.float32)
                + jnp.where(edge, 0.0, inter.astype(jnp.float32))
            )
            result[t] = finished(stream, conv, block, mid_scale_ref, mid_shift_ref, point_ref)
            copies.append(
                pltpu.make_async_copy(result.at[t], out_ref.at[first + t, target], sems.at[t])
            )
            copies[-1].start()
        for copy in copies:
            copy.wait()

    both_ways(body)


def swaps(groups, devices):
    intra, inter = [], []
    for g in range(groups):
        base = g * devices
        intra += [(base + i, base + i + 1) for i in range(0, devices - 1, 2)]
        inter += [(base + i, base + i + 1) for i in range(1, devices - 1, 2)]
    for g in range(0, groups - 1, 2):
        for end in (0, devices - 1):
            inter.append((g * devices + end, (g + 1) * devices + end))
    return tuple(pairs + [(b, a) for a, b in pairs] for pairs in (intra, inter))


def local(
    tower_in, first_norm_scale, first_norm_shift, conv_weight, mid_scale, second_norm_shift, point_weight
):
    tracks, rows, channels = tower_in.shape
    blocks, _, _, filters = conv_weight.shape
    intra_pairs, inter_pairs = swaps(lax.axis_size("groups"), lax.axis_size("seq"))
    spans = [FIRST_DILATION * 2**b for b in range(blocks)]
    vmem = pl.BlockSpec(memory_space=pltpu.VMEM)
    hbm = pl.BlockSpec(memory_space=pltpu.HBM)
    params = pltpu.CompilerParams(vmem_limit_bytes=32 * MIB)
    norms = (first_norm_scale, first_norm_shift)
    mids = (mid_scale, second_norm_shift, point_weight)

    def cross(value):
        return lax.ppermute(value, ("groups", "seq"), inter_pairs)

    def across(value):
        return lax.ppermute(value, ("groups", "seq"), intra_pairs)

    def cost(count, conv=1, point=1, part=tracks):
        flops = 20 * part * count * channels * filters * (TAPS * conv + point)
        return pl.CostEstimate(flops=flops, bytes_accessed=flops // 1000, transcendentals=0)

    def halo(count, part=tracks):
        return jax.ShapeDtypeStruct((part, count, filters), jnp.bfloat16)

    def sums(count, part=tracks):
        return jax.ShapeDtypeStruct((part, count, filters), jnp.float32)

    def step(block, q, streams, terms, sends, keep, after=(), first=0, part=tracks):
        plan = (
            block, q, first,
            [r for r, _ in streams], [(r, c) for r, c, _ in terms], sends, keep,
        )
        arrays = [a for _, a in streams] + [a for _, _, a in terms]
        count = q[1] - q[0]
        made = pl.pallas_call(
            functools.partial(step_kernel, plan),
            in_specs=[vmem] * (len(arrays) + 6 + len(after)),
            out_specs=[vmem] * (1 + len(sends) + len(keep)),
            out_shape=[jax.ShapeDtypeStruct((part, count, channels), jnp.bfloat16)]
            + [halo(r[1] - r[0], part) for _, r in sends]
            + [sums(r[1] - r[0], part) for r, _ in keep],
            compiler_params=params,
            cost_estimate=cost(count, part=part),
        )(*arrays, *mids, *norms, conv_weight, *after)
        return made[0], made[1 : 1 + len(sends)], made[1 + len(sends) :]

    everything = (0, rows)
    one, two, three, four = spans

    far = [
        pltpu.with_memory_space_constraint(x, pltpu.HBM)
        for x in (tower_in, first_norm_scale, first_norm_shift, conv_weight)
    ]
    intra, inter = pl.pallas_call(
        functools.partial(edge_kernel, one),
        in_specs=[hbm] * 4,
        out_specs=[vmem] * 2,
        out_shape=[halo(one)] * 2,
        scratch_shapes=[pltpu.VMEM((tracks, one, channels), jnp.bfloat16)] * 2
        + [pltpu.VMEM(first_norm_scale.shape, jnp.float32)] * 2
        + [pltpu.VMEM((2, channels, filters), jnp.bfloat16), pltpu.SemaphoreType.DMA((6,))],
        compiler_params=params,
        cost_estimate=cost(one, point=0),
    )(*far)
    inter_0, intra_0 = cross(inter), across(intra)
    local_0 = pl.pallas_call(
        functools.partial(entry_kernel, one),
        in_specs=[vmem] * 4,
        out_specs=vmem,
        out_shape=sums(rows),
        compiler_params=params,
        cost_estimate=cost(rows, point=0),
    )(tower_in, *norms, conv_weight)

    rest = (two, rows)
    stream_1f, (inter,), (here_1f, inn_1f) = step(
        0, (0, two),
        [(everything, tower_in)],
        [(everything, False, local_0), ((0, one), True, inter_0)],
        [("out", (0, two))],
        [((0, two), [("here", (0, two), 0)]), ((two, 2 * two), [("inn", (0, two), two)])],
    )
    inter_1 = cross(inter)
    stream_1n, (intra,), (local_1n,) = step(
        0, rest,
        [(everything, tower_in)],
        [(everything, False, local_0), ((rows - one, rows), False, intra_0)],
        [("inn", (rows - two, rows))],
        [
            (
                everything,
                [
                    ("here", rest, 0),
                    ("out", rest, -two),
                    ("inn", (two, rows - two), two),
                ],
            )
        ],
        after=(here_1f,),
    )
    intra_1 = across(intra)
    streams = [((0, two), stream_1f), (rest, stream_1n)]

    middle, near = (two, three), (three, rows)
    stream_2m, (inter,), (here_2m, inn_2m) = step(
        1, middle,
        streams[1:],
        [(everything, False, local_1n), ((two, 2 * two), False, inn_1f)],
        [("out", middle)],
        [(middle, [("here", middle, 0)]), ((two + three, rows), [("inn", middle, three)])],
    )
    inter_2m = cross(inter)
    stream_2n, (intra,), (local_2n,) = step(
        1, near,
        streams[1:],
        [(everything, False, local_1n), ((rows - two, rows), False, intra_1)],
        [("inn", near)],
        [(everything, [("here", near, 0), ("out", near, -three)])],
        after=(here_2m,),
    )
    intra_2 = across(intra)
    stream_2f, (inter,), (here_2f, inn_2f) = step(
        1, (0, two),
        streams[:1],
        [
            (everything, False, local_1n),
            ((0, two), False, here_1f),
            ((0, two), True, inter_1),
        ],
        [("out", (0, two))],
        [((0, two), [("here", (0, two), 0)]), ((three, three + two), [("inn", (0, two), three)])],
        after=(local_2n,),
    )
    inter_2f = cross(inter)

    stream_3n, (inter, intra), (local_3n,) = step(
        2, near,
        [(near, stream_2n)],
        [
            (everything, False, local_2n),
            ((three, three + two), False, inn_2f),
            ((two + three, rows), False, inn_2m),
            (near, False, intra_2),
        ],
        [("out", near), ("inn", near)],
        [(near, [("here", near, 0)])],
    )
    inter_3n, intra_3n = cross(inter), across(intra)
    parts = [(0, tracks // 2), (tracks // 2, tracks - tracks // 2)]
    ends, after = [], (local_3n,)
    for first, part in parts:
        stream_3f, (inter, intra), (local_3f,) = step(
            2, (0, three),
            [((0, two), stream_2f), (middle, stream_2m)],
            [
                (everything, False, local_2n),
                ((0, two), False, here_2f),
                (middle, False, here_2m),
                ((0, two), True, inter_2m),
                (middle, True, inter_2f),
            ],
            [("out", (0, three)), ("inn", (0, three))],
            [((0, three), [("here", (0, three), 0)])],
            after=after, first=first, part=part,
        )
        after = (local_3f,)
        ends.append((stream_3f, local_3f, cross(inter), across(intra)))

    far_ends, near_ends = [], []
    for (first, part), (stream_3f, local_3f, inter, intra) in zip(parts, ends):
        far_ends.append(
            ((0, three), first, part, (0, 0, first, first), (stream_3f, local_3f, intra_3n, inter_3n))
        )
        near_ends.append(
            (near, first, part, (first, first, 0, 0), (stream_3n, local_3n, intra, inter))
        )
    out = []
    for q, first, part, bases, arrays in far_ends + near_ends:
        count = q[1] - q[0]
        out = [
            pl.pallas_call(
                functools.partial(last_kernel, blocks - 1, q, rows, first, bases),
                in_specs=[vmem] * 7 + [hbm] * len(out),
                out_specs=hbm,
                out_shape=jax.ShapeDtypeStruct(tower_in.shape, jnp.bfloat16),
                scratch_shapes=[
                    pltpu.VMEM((part, count, channels), jnp.bfloat16),
                    pltpu.SemaphoreType.DMA((part,)),
                ],
                input_output_aliases={7: 0} if out else {},
                compiler_params=params,
                cost_estimate=cost(count, conv=0, part=part),
            )(*arrays, *mids, *out)
        ]
    return out[0]


def solution(mesh):
    placed = (P("groups", "seq", None), P(), P(), P(), P(), P(), P())
    return jax.shard_map(
        local, mesh=mesh, in_specs=placed, out_specs=P("groups", "seq", None), check_vma=False
    )
```

```python
import functools

import jax
import jax.numpy as jnp
from jax import lax
from jax.experimental import pallas as pl
from jax.experimental.pallas import tpu as pltpu
from jax.sharding import PartitionSpec as P

FIRST_DILATION = 32
MIB = 1024 * 1024
TAPS = 3


def place():
    index = lax.axis_index("seq")
    even = lax.rem(index, 2) == 0
    edge = jnp.logical_or(index == 0, index == lax.axis_size("seq") - 1)
    return even, edge


def both_ways(body):
    even, edge = place()
    pl.when(even)(lambda: body(True, edge))
    pl.when(jnp.logical_not(even))(lambda: body(False, edge))


def span_of(q, within, even):
    if even:
        return slice(q[0] - within[0], q[1] - within[0])
    return slice(within[1] - q[1], within[1] - q[0])


def value_term(value, within, even):
    return within, lambda q: value[span_of(q, within, even)]


def ref_term(ref, t, within, even, drop=None):
    def get(q):
        part = ref[t, span_of(q, within, even)].astype(jnp.float32)
        return part if drop is None else jnp.where(drop, 0.0, part)

    return within, get


def assemble(q, terms, even):
    cuts = sorted({q[0], q[1], *(min(max(c, q[0]), q[1]) for rows, _ in terms for c in rows)})
    pieces = []
    for low, high in zip(cuts[:-1], cuts[1:]):
        total = None
        for rows, get in terms:
            if rows[0] <= low and high <= rows[1]:
                part = get((low, high))
                total = part if total is None else total + part
        pieces.append(total)
    if not even:
        pieces = pieces[::-1]
    return pieces[0] if len(pieces) == 1 else jnp.concatenate(pieces, axis=0)


def moved(value, within, q, by, even):
    return (q[0] + by, q[1] + by), lambda to: value[
        span_of((to[0] - by, to[1] - by), within, even)
    ]


def normed_of(stream, scale, shift):
    return jnp.maximum(stream.astype(jnp.float32) * scale + shift, 0.0).astype(jnp.bfloat16)


def products_of(stream, block, even, scale_ref, shift_ref, weight_ref):
    filters = weight_ref.shape[-1]
    normed = normed_of(stream, scale_ref[block : block + 1], shift_ref[block : block + 1])
    weight = jnp.concatenate([weight_ref[block, k] for k in range(TAPS)], axis=1)
    product = jnp.dot(normed, weight, preferred_element_type=jnp.float32)
    behind, here, ahead = (product[:, k * filters : (k + 1) * filters] for k in range(TAPS))
    return (ahead, here, behind) if even else (behind, here, ahead)


def finished(stream, conv, block, scale_ref, shift_ref, point_ref):
    middle = jnp.maximum(
        conv * scale_ref[block : block + 1] + shift_ref[block : block + 1], 0.0
    ).astype(jnp.bfloat16)
    update = jnp.dot(middle, point_ref[block], preferred_element_type=jnp.float32)
    return (stream.astype(jnp.float32) + update).astype(jnp.bfloat16)


def stacked(parts):
    return jnp.concatenate(parts, axis=0)


def edge_kernel(
    span, tower_ref, scale_ref, shift_ref, weight_ref, inter_ref, part, scale, shift, weight, sems
):
    tracks, rows, channels = tower_ref.shape

    def body(even, edge):
        source = tower_ref.at[:, span_of((0, span), (0, rows), even)]
        copies = [
            pltpu.make_async_copy(source, target, sems.at[i])
            for i, (source, target) in enumerate(
                [
                    (source, part),
                    (weight_ref.at[0, TAPS - 1 if even else 0], weight),
                    (scale_ref, scale),
                    (shift_ref, shift),
                ]
            )
        ]
        for copy in copies:
            copy.start()
        for i in (2, 3, 0):
            copies[i].wait()
        normed = normed_of(part[...].reshape(tracks * span, channels), scale[0:1], shift[0:1])
        copies[1].wait()
        inter_ref[...] = (
            jnp.dot(normed, weight[...], preferred_element_type=jnp.float32)
            .astype(jnp.bfloat16)
            .reshape(inter_ref.shape)
        )

    both_ways(body)


def entry_kernel(span, tower_ref, scale_ref, shift_ref, weight_ref, local_ref, intra_ref):
    tracks, rows, channels = tower_ref.shape
    everything = (0, rows)

    def body(even, edge):
        out, here, inn = products_of(
            tower_ref[...].reshape(tracks * rows, channels),
            0, even, scale_ref, shift_ref, weight_ref,
        )
        for t in range(tracks):
            own = slice(t * rows, (t + 1) * rows)
            intra_ref[t] = inn[own][span_of((rows - span, rows), everything, even)].astype(
                jnp.bfloat16
            )
            local_ref[t] = assemble(
                everything,
                [
                    value_term(here[own], everything, even),
                    moved(out[own], everything, (span, rows), -span, even),
                    moved(inn[own], everything, (0, rows - span), span, even),
                ],
                even,
            )

    both_ways(body)


def step_kernel(plan, *refs):
    block, q, first, streams, terms, sends, keep = plan
    refs = list(refs)
    take = lambda n: [refs.pop(0) for _ in range(n)]
    stream_refs, term_refs = take(len(streams)), take(len(terms))
    mid_scale_ref, mid_shift_ref, point_ref = take(3)
    scale_ref, shift_ref, weight_ref = take(3)
    refs = refs[-(1 + len(sends) + len(keep)) :]
    out_ref = refs.pop(0)
    send_refs, keep_refs = take(len(sends)), take(len(keep))
    tracks, count = out_ref.shape[0], q[1] - q[0]

    def body(even, edge):
        conv = stacked(
            [
                assemble(
                    q,
                    [
                        ref_term(ref, first + t, rows, even, edge if crossed else None)
                        for ref, (rows, crossed) in zip(term_refs, terms)
                    ],
                    even,
                )
                for t in range(tracks)
            ]
        )
        stream = stacked(
            [
                assemble_stream(q, stream_refs, streams, first + t, even)
                for t in range(tracks)
            ]
        )
        stream = finished(stream, conv, block, mid_scale_ref, mid_shift_ref, point_ref)
        out_ref[...] = stream.reshape(out_ref.shape)
        named = dict(
            zip(
                ("out", "here", "inn"),
                products_of(stream, block + 1, even, scale_ref, shift_ref, weight_ref),
            )
        )
        for t in range(tracks):
            own = slice(t * count, (t + 1) * count)
            for ref, (name, rows) in zip(send_refs, sends):
                ref[t] = named[name][own][span_of(rows, q, even)].astype(jnp.bfloat16)
            for ref, (rows, parts) in zip(keep_refs, keep):
                ref[t] = assemble(
                    rows,
                    [moved(named[name][own], q, part, by, even) for name, part, by in parts],
                    even,
                )

    both_ways(body)


def assemble_stream(q, stream_refs, streams, t, even):
    pieces = []
    for ref, within in zip(stream_refs, streams):
        low, high = max(q[0], within[0]), min(q[1], within[1])
        if low < high:
            pieces.append(ref[t, span_of((low, high), within, even)])
    if not even:
        pieces = pieces[::-1]
    return pieces[0] if len(pieces) == 1 else jnp.concatenate(pieces, axis=0)


def last_kernel(
    block, q, rows, first, bases, stream_ref, local_ref, intra_ref, inter_ref, *refs
):
    mid_scale_ref, mid_shift_ref, point_ref = refs[:3]
    out_ref, result, sems = refs[-3:]

    def body(even, edge):
        target = span_of(q, (0, rows), even)
        copies = []
        for t in range(result.shape[0]):
            stream, local, intra, inter = (
                ref[base + t]
                for ref, base in zip((stream_ref, local_ref, intra_ref, inter_ref), bases)
            )
            conv = (
                local
                + intra.astype(jnp.float32)
                + jnp.where(edge, 0.0, inter.astype(jnp.float32))
            )
            result[t] = finished(stream, conv, block, mid_scale_ref, mid_shift_ref, point_ref)
            copies.append(
                pltpu.make_async_copy(result.at[t], out_ref.at[first + t, target], sems.at[t])
            )
            copies[-1].start()
        for copy in copies:
            copy.wait()

    both_ways(body)


def swaps(groups, devices):
    intra, inter = [], []
    for g in range(groups):
        base = g * devices
        intra += [(base + i, base + i + 1) for i in range(0, devices - 1, 2)]
        inter += [(base + i, base + i + 1) for i in range(1, devices - 1, 2)]
    for g in range(0, groups - 1, 2):
        for end in (0, devices - 1):
            inter.append((g * devices + end, (g + 1) * devices + end))
    return tuple(pairs + [(b, a) for a, b in pairs] for pairs in (intra, inter))


def local(
    tower_in, first_norm_scale, first_norm_shift, conv_weight, mid_scale, second_norm_shift, point_weight
):
    tracks, rows, channels = tower_in.shape
    blocks, _, _, filters = conv_weight.shape
    intra_pairs, inter_pairs = swaps(lax.axis_size("groups"), lax.axis_size("seq"))
    spans = [FIRST_DILATION * 2**b for b in range(blocks)]
    vmem = pl.BlockSpec(memory_space=pltpu.VMEM)
    hbm = pl.BlockSpec(memory_space=pltpu.HBM)
    params = pltpu.CompilerParams(vmem_limit_bytes=32 * MIB)
    norms = (first_norm_scale, first_norm_shift)
    mids = (mid_scale, second_norm_shift, point_weight)

    def cross(value):
        return lax.ppermute(value, ("groups", "seq"), inter_pairs)

    def across(value):
        return lax.ppermute(value, ("groups", "seq"), intra_pairs)

    def cost(count, conv=1, point=1, part=tracks):
        flops = 20 * part * count * channels * filters * (TAPS * conv + point)
        return pl.CostEstimate(flops=flops, bytes_accessed=flops // 1000, transcendentals=0)

    def halo(count, part=tracks):
        return jax.ShapeDtypeStruct((part, count, filters), jnp.bfloat16)

    def sums(count, part=tracks):
        return jax.ShapeDtypeStruct((part, count, filters), jnp.float32)

    def step(block, q, streams, terms, sends, keep, after=(), first=0, part=tracks):
        plan = (
            block, q, first,
            [r for r, _ in streams], [(r, c) for r, c, _ in terms], sends, keep,
        )
        arrays = [a for _, a in streams] + [a for _, _, a in terms]
        count = q[1] - q[0]
        made = pl.pallas_call(
            functools.partial(step_kernel, plan),
            in_specs=[vmem] * (len(arrays) + 6 + len(after)),
            out_specs=[vmem] * (1 + len(sends) + len(keep)),
            out_shape=[jax.ShapeDtypeStruct((part, count, channels), jnp.bfloat16)]
            + [halo(r[1] - r[0], part) for _, r in sends]
            + [sums(r[1] - r[0], part) for r, _ in keep],
            compiler_params=params,
            cost_estimate=cost(count, part=part),
        )(*arrays, *mids, *norms, conv_weight, *after)
        return made[0], made[1 : 1 + len(sends)], made[1 + len(sends) :]

    everything = (0, rows)
    one, two, three, four = spans

    far = [
        pltpu.with_memory_space_constraint(x, pltpu.HBM)
        for x in (tower_in, first_norm_scale, first_norm_shift, conv_weight)
    ]
    inter = pl.pallas_call(
        functools.partial(edge_kernel, one),
        in_specs=[hbm] * 4,
        out_specs=vmem,
        out_shape=halo(one),
        scratch_shapes=[pltpu.VMEM((tracks, one, channels), jnp.bfloat16)]
        + [pltpu.VMEM(first_norm_scale.shape, jnp.float32)] * 2
        + [pltpu.VMEM((channels, filters), jnp.bfloat16), pltpu.SemaphoreType.DMA((4,))],
        compiler_params=params,
        cost_estimate=cost(one, point=0),
    )(*far)
    inter_0 = cross(inter)
    local_0, intra = pl.pallas_call(
        functools.partial(entry_kernel, one),
        in_specs=[vmem] * 4,
        out_specs=[vmem] * 2,
        out_shape=[sums(rows), halo(one)],
        compiler_params=params,
        cost_estimate=cost(rows, point=0),
    )(tower_in, *norms, conv_weight)
    intra_0 = across(intra)

    rest = (two, rows)
    stream_1f, (inter,), (here_1f, inn_1f) = step(
        0, (0, two),
        [(everything, tower_in)],
        [(everything, False, local_0), ((0, one), True, inter_0)],
        [("out", (0, two))],
        [((0, two), [("here", (0, two), 0)]), ((two, 2 * two), [("inn", (0, two), two)])],
    )
    inter_1 = cross(inter)
    stream_1n, (intra,), (local_1n,) = step(
        0, rest,
        [(everything, tower_in)],
        [(everything, False, local_0), ((rows - one, rows), False, intra_0)],
        [("inn", (rows - two, rows))],
        [
            (
                everything,
                [
                    ("here", rest, 0),
                    ("out", rest, -two),
                    ("inn", (two, rows - two), two),
                ],
            )
        ],
        after=(here_1f,),
    )
    intra_1 = across(intra)
    streams = [((0, two), stream_1f), (rest, stream_1n)]

    middle, near = (two, three), (three, rows)
    stream_2m, (inter,), (here_2m, inn_2m) = step(
        1, middle,
        streams[1:],
        [(everything, False, local_1n), ((two, 2 * two), False, inn_1f)],
        [("out", middle)],
        [(middle, [("here", middle, 0)]), ((two + three, rows), [("inn", middle, three)])],
    )
    inter_2m = cross(inter)
    stream_2n, (intra,), (local_2n,) = step(
        1, near,
        streams[1:],
        [(everything, False, local_1n), ((rows - two, rows), False, intra_1)],
        [("inn", near)],
        [(everything, [("here", near, 0), ("out", near, -three)])],
        after=(here_2m,),
    )
    intra_2 = across(intra)
    stream_2f, (inter,), (here_2f, inn_2f) = step(
        1, (0, two),
        streams[:1],
        [
            (everything, False, local_1n),
            ((0, two), False, here_1f),
            ((0, two), True, inter_1),
        ],
        [("out", (0, two))],
        [((0, two), [("here", (0, two), 0)]), ((three, three + two), [("inn", (0, two), three)])],
        after=(local_2n,),
    )
    inter_2f = cross(inter)

    stream_3n, (inter, intra), (local_3n,) = step(
        2, near,
        [(near, stream_2n)],
        [
            (everything, False, local_2n),
            ((three, three + two), False, inn_2f),
            ((two + three, rows), False, inn_2m),
            (near, False, intra_2),
        ],
        [("out", near), ("inn", near)],
        [(near, [("here", near, 0)])],
    )
    inter_3n, intra_3n = cross(inter), across(intra)
    parts = [(0, tracks // 2), (tracks // 2, tracks - tracks // 2)]
    ends, after = [], (local_3n,)
    for first, part in parts:
        stream_3f, (inter, intra), (local_3f,) = step(
            2, (0, three),
            [((0, two), stream_2f), (middle, stream_2m)],
            [
                (everything, False, local_2n),
                ((0, two), False, here_2f),
                (middle, False, here_2m),
                ((0, two), True, inter_2m),
                (middle, True, inter_2f),
            ],
            [("out", (0, three)), ("inn", (0, three))],
            [((0, three), [("here", (0, three), 0)])],
            after=after, first=first, part=part,
        )
        after = (local_3f,)
        ends.append((stream_3f, local_3f, cross(inter), across(intra)))

    far_ends, near_ends = [], []
    for (first, part), (stream_3f, local_3f, inter, intra) in zip(parts, ends):
        far_ends.append(
            ((0, three), first, part, (0, 0, first, first), (stream_3f, local_3f, intra_3n, inter_3n))
        )
        near_ends.append(
            (near, first, part, (first, first, 0, 0), (stream_3n, local_3n, intra, inter))
        )
    out = []
    for q, first, part, bases, arrays in far_ends + near_ends:
        count = q[1] - q[0]
        out = [
            pl.pallas_call(
                functools.partial(last_kernel, blocks - 1, q, rows, first, bases),
                in_specs=[vmem] * 7 + [hbm] * len(out),
                out_specs=hbm,
                out_shape=jax.ShapeDtypeStruct(tower_in.shape, jnp.bfloat16),
                scratch_shapes=[
                    pltpu.VMEM((part, count, channels), jnp.bfloat16),
                    pltpu.SemaphoreType.DMA((part,)),
                ],
                input_output_aliases={7: 0} if out else {},
                compiler_params=params,
                cost_estimate=cost(count, conv=0, part=part),
            )(*arrays, *mids, *out)
        ]
    return out[0]


def solution(mesh):
    placed = (P("groups", "seq", None), P(), P(), P(), P(), P(), P())
    return jax.shard_map(
        local, mesh=mesh, in_specs=placed, out_specs=P("groups", "seq", None), check_vma=False
    )
```

```python
import functools

import jax
import jax.numpy as jnp
from jax import lax
from jax.experimental import pallas as pl
from jax.experimental.pallas import tpu as pltpu
from jax.sharding import PartitionSpec as P

FIRST_DILATION = 32
MIB = 1024 * 1024
TAPS = 3


def place():
    index = lax.axis_index("seq")
    even = lax.rem(index, 2) == 0
    edge = jnp.logical_or(index == 0, index == lax.axis_size("seq") - 1)
    return even, edge


def both_ways(body):
    even, edge = place()
    pl.when(even)(lambda: body(True, edge))
    pl.when(jnp.logical_not(even))(lambda: body(False, edge))


def span_of(q, within, even):
    if even:
        return slice(q[0] - within[0], q[1] - within[0])
    return slice(within[1] - q[1], within[1] - q[0])


def value_term(value, within, even):
    return within, lambda q: value[span_of(q, within, even)]


def ref_term(ref, t, within, even, drop=None):
    def get(q):
        part = ref[t, span_of(q, within, even)].astype(jnp.float32)
        return part if drop is None else jnp.where(drop, 0.0, part)

    return within, get


def assemble(q, terms, even):
    cuts = sorted({q[0], q[1], *(min(max(c, q[0]), q[1]) for rows, _ in terms for c in rows)})
    pieces = []
    for low, high in zip(cuts[:-1], cuts[1:]):
        total = None
        for rows, get in terms:
            if rows[0] <= low and high <= rows[1]:
                part = get((low, high))
                total = part if total is None else total + part
        pieces.append(total)
    if not even:
        pieces = pieces[::-1]
    return pieces[0] if len(pieces) == 1 else jnp.concatenate(pieces, axis=0)


def moved(value, within, q, by, even):
    return (q[0] + by, q[1] + by), lambda to: value[
        span_of((to[0] - by, to[1] - by), within, even)
    ]


def normed_of(stream, scale, shift):
    return jnp.maximum(stream.astype(jnp.float32) * scale + shift, 0.0).astype(jnp.bfloat16)


def products_of(stream, block, even, names, scale_ref, shift_ref, weight_ref):
    filters = weight_ref.shape[-1]
    normed = normed_of(stream, scale_ref[block : block + 1], shift_ref[block : block + 1])
    order = ("inn", "here", "out") if even else ("out", "here", "inn")
    chosen = [(k, name) for k, name in enumerate(order) if name in names]
    weight = jnp.concatenate([weight_ref[block, k] for k, _ in chosen], axis=1)
    product = jnp.dot(normed, weight, preferred_element_type=jnp.float32)
    return {
        name: product[:, i * filters : (i + 1) * filters] for i, (_, name) in enumerate(chosen)
    }


def finished(stream, conv, block, scale_ref, shift_ref, point_ref):
    middle = jnp.maximum(
        conv * scale_ref[block : block + 1] + shift_ref[block : block + 1], 0.0
    ).astype(jnp.bfloat16)
    update = jnp.dot(middle, point_ref[block], preferred_element_type=jnp.float32)
    return (stream.astype(jnp.float32) + update).astype(jnp.bfloat16)


def stacked(parts):
    return jnp.concatenate(parts, axis=0)


def edge_kernel(
    span, tower_ref, scale_ref, shift_ref, weight_ref, inter_ref, part, scale, shift, weight, sems
):
    tracks, rows, channels = tower_ref.shape

    def body(even, edge):
        source = tower_ref.at[:, span_of((0, span), (0, rows), even)]
        copies = [
            pltpu.make_async_copy(source, target, sems.at[i])
            for i, (source, target) in enumerate(
                [
                    (source, part),
                    (weight_ref.at[0, TAPS - 1 if even else 0], weight),
                    (scale_ref, scale),
                    (shift_ref, shift),
                ]
            )
        ]
        for copy in copies:
            copy.start()
        for i in (2, 3, 0):
            copies[i].wait()
        normed = normed_of(part[...].reshape(tracks * span, channels), scale[0:1], shift[0:1])
        copies[1].wait()
        inter_ref[...] = (
            jnp.dot(normed, weight[...], preferred_element_type=jnp.float32)
            .astype(jnp.bfloat16)
            .reshape(inter_ref.shape)
        )

    both_ways(body)


def entry_kernel(span, tower_ref, scale_ref, shift_ref, weight_ref, local_ref, intra_ref):
    tracks, rows, channels = tower_ref.shape
    everything = (0, rows)

    def body(even, edge):
        named = products_of(
            tower_ref[...].reshape(tracks * rows, channels),
            0, even, ("out", "here", "inn"), scale_ref, shift_ref, weight_ref,
        )
        out, here, inn = named["out"], named["here"], named["inn"]
        for t in range(tracks):
            own = slice(t * rows, (t + 1) * rows)
            intra_ref[t] = inn[own][span_of((rows - span, rows), everything, even)].astype(
                jnp.bfloat16
            )
            local_ref[t] = assemble(
                everything,
                [
                    value_term(here[own], everything, even),
                    moved(out[own], everything, (span, rows), -span, even),
                    moved(inn[own], everything, (0, rows - span), span, even),
                ],
                even,
            )

    both_ways(body)


def step_kernel(plan, *refs):
    block, q, first, streams, terms, sends, keep, late = plan
    refs = list(refs)
    take = lambda n: [refs.pop(0) for _ in range(n)]
    stream_refs, term_refs, late_refs = take(len(streams)), take(len(terms)), take(len(late))
    mid_scale_ref, mid_shift_ref, point_ref = take(3)
    scale_ref, shift_ref, weight_ref = take(3)
    refs = refs[-(1 + len(sends) + len(keep) + sum(len(kept) for _, kept in late)) :]
    out_ref = refs.pop(0)
    send_refs, keep_refs = take(len(sends)), take(len(keep))
    late_keep_refs = [take(len(kept)) for _, kept in late]
    tracks, count = out_ref.shape[0], q[1] - q[0]

    def body(even, edge):
        conv = stacked(
            [
                assemble(
                    q,
                    [
                        ref_term(ref, first + t, rows, even, edge if crossed else None)
                        for ref, (rows, crossed) in zip(term_refs, terms)
                    ],
                    even,
                )
                for t in range(tracks)
            ]
        )
        stream = stacked(
            [
                assemble_stream(q, stream_refs, streams, first + t, even)
                for t in range(tracks)
            ]
        )
        stream = finished(stream, conv, block, mid_scale_ref, mid_shift_ref, point_ref)
        out_ref[...] = stream.reshape(out_ref.shape)
        names = {name for name, _ in sends} | {name for _, parts in keep for name, _, _ in parts}
        named = products_of(stream, block + 1, even, names, scale_ref, shift_ref, weight_ref)
        for t in range(tracks):
            own = slice(t * count, (t + 1) * count)
            for ref, (name, rows) in zip(send_refs, sends):
                ref[t] = named[name][own][span_of(rows, q, even)].astype(jnp.bfloat16)
        store(named, q, keep_refs, keep, even)
        for ref, kept_refs, (rows, kept) in zip(late_refs, late_keep_refs, late):
            stream = ref[...].reshape(-1, ref.shape[-1])
            names = {name for _, parts in kept for name, _, _ in parts}
            named = products_of(stream, block + 1, even, names, scale_ref, shift_ref, weight_ref)
            store(named, rows, kept_refs, kept, even)

    def store(named, q, keep_refs, keep, even):
        count = q[1] - q[0]
        for t in range(tracks):
            own = slice(t * count, (t + 1) * count)
            for ref, (rows, parts) in zip(keep_refs, keep):
                ref[t] = assemble(
                    rows,
                    [moved(named[name][own], q, part, by, even) for name, part, by in parts],
                    even,
                )

    both_ways(body)


def assemble_stream(q, stream_refs, streams, t, even):
    pieces = []
    for ref, within in zip(stream_refs, streams):
        low, high = max(q[0], within[0]), min(q[1], within[1])
        if low < high:
            pieces.append(ref[t, span_of((low, high), within, even)])
    if not even:
        pieces = pieces[::-1]
    return pieces[0] if len(pieces) == 1 else jnp.concatenate(pieces, axis=0)


def last_kernel(
    block, q, rows, first, bases, stream_ref, local_ref, intra_ref, inter_ref, *refs
):
    mid_scale_ref, mid_shift_ref, point_ref = refs[:3]
    out_ref, result, sems = refs[-3:]

    def body(even, edge):
        target = span_of(q, (0, rows), even)
        copies = []
        for t in range(result.shape[0]):
            stream, local, intra, inter = (
                ref[base + t]
                for ref, base in zip((stream_ref, local_ref, intra_ref, inter_ref), bases)
            )
            conv = (
                local
                + intra.astype(jnp.float32)
                + jnp.where(edge, 0.0, inter.astype(jnp.float32))
            )
            result[t] = finished(stream, conv, block, mid_scale_ref, mid_shift_ref, point_ref)
            copies.append(
                pltpu.make_async_copy(result.at[t], out_ref.at[first + t, target], sems.at[t])
            )
            copies[-1].start()
        for copy in copies:
            copy.wait()

    both_ways(body)


def swaps(groups, devices):
    intra, inter = [], []
    for g in range(groups):
        base = g * devices
        intra += [(base + i, base + i + 1) for i in range(0, devices - 1, 2)]
        inter += [(base + i, base + i + 1) for i in range(1, devices - 1, 2)]
    for g in range(0, groups - 1, 2):
        for end in (0, devices - 1):
            inter.append((g * devices + end, (g + 1) * devices + end))
    return tuple(pairs + [(b, a) for a, b in pairs] for pairs in (intra, inter))


def local(
    tower_in, first_norm_scale, first_norm_shift, conv_weight, mid_scale, second_norm_shift, point_weight
):
    tracks, rows, channels = tower_in.shape
    blocks, _, _, filters = conv_weight.shape
    intra_pairs, inter_pairs = swaps(lax.axis_size("groups"), lax.axis_size("seq"))
    spans = [FIRST_DILATION * 2**b for b in range(blocks)]
    vmem = pl.BlockSpec(memory_space=pltpu.VMEM)
    hbm = pl.BlockSpec(memory_space=pltpu.HBM)
    params = pltpu.CompilerParams(vmem_limit_bytes=32 * MIB)
    norms = (first_norm_scale, first_norm_shift)
    mids = (mid_scale, second_norm_shift, point_weight)

    def cross(value):
        return lax.ppermute(value, ("groups", "seq"), inter_pairs)

    def across(value):
        return lax.ppermute(value, ("groups", "seq"), intra_pairs)

    def cost(count, conv=1, point=1, part=tracks):
        flops = 20 * part * count * channels * filters * (TAPS * conv + point)
        return pl.CostEstimate(flops=flops, bytes_accessed=flops // 1000, transcendentals=0)

    def halo(count, part=tracks):
        return jax.ShapeDtypeStruct((part, count, filters), jnp.bfloat16)

    def sums(count, part=tracks):
        return jax.ShapeDtypeStruct((part, count, filters), jnp.float32)

    def step(block, q, streams, terms, sends, keep, after=(), first=0, part=tracks, late=()):
        plan = (
            block, q, first,
            [r for r, _ in streams], [(r, c) for r, c, _ in terms], sends, keep,
            [(r, kept) for r, _, kept in late],
        )
        arrays = [a for _, a in streams] + [a for _, _, a in terms] + [a for _, a, _ in late]
        kept_rows = [r for r, _ in keep] + [r for _, _, kept in late for r, _ in kept]
        count = q[1] - q[0]
        made = pl.pallas_call(
            functools.partial(step_kernel, plan),
            in_specs=[vmem] * (len(arrays) + 6 + len(after)),
            out_specs=[vmem] * (1 + len(sends) + len(kept_rows)),
            out_shape=[jax.ShapeDtypeStruct((part, count, channels), jnp.bfloat16)]
            + [halo(r[1] - r[0], part) for _, r in sends]
            + [sums(r[1] - r[0], part) for r in kept_rows],
            compiler_params=params,
            cost_estimate=cost(count, part=part),
        )(*arrays, *mids, *norms, conv_weight, *after)
        return made[0], made[1 : 1 + len(sends)], made[1 + len(sends) :]

    everything = (0, rows)
    one, two, three, four = spans

    far = [
        pltpu.with_memory_space_constraint(x, pltpu.HBM)
        for x in (tower_in, first_norm_scale, first_norm_shift, conv_weight)
    ]
    inter = pl.pallas_call(
        functools.partial(edge_kernel, one),
        in_specs=[hbm] * 4,
        out_specs=vmem,
        out_shape=halo(one),
        scratch_shapes=[pltpu.VMEM((tracks, one, channels), jnp.bfloat16)]
        + [pltpu.VMEM(first_norm_scale.shape, jnp.float32)] * 2
        + [pltpu.VMEM((channels, filters), jnp.bfloat16), pltpu.SemaphoreType.DMA((4,))],
        compiler_params=params,
        cost_estimate=cost(one, point=0),
    )(*far)
    inter_0 = cross(inter)
    local_0, intra = pl.pallas_call(
        functools.partial(entry_kernel, one),
        in_specs=[vmem] * 4,
        out_specs=[vmem] * 2,
        out_shape=[sums(rows), halo(one)],
        compiler_params=params,
        cost_estimate=cost(rows, point=0),
    )(tower_in, *norms, conv_weight)
    intra_0 = across(intra)

    rest = (two, rows)
    stream_1f, (inter,), (here_1f, inn_1f) = step(
        0, (0, two),
        [(everything, tower_in)],
        [(everything, False, local_0), ((0, one), True, inter_0)],
        [("out", (0, two))],
        [((0, two), [("here", (0, two), 0)]), ((two, 2 * two), [("inn", (0, two), two)])],
    )
    inter_1 = cross(inter)
    stream_1n, (intra,), (local_1n,) = step(
        0, rest,
        [(everything, tower_in)],
        [(everything, False, local_0), ((rows - one, rows), False, intra_0)],
        [("inn", (rows - two, rows))],
        [
            (
                everything,
                [
                    ("here", rest, 0),
                    ("out", rest, -two),
                    ("inn", (two, rows - two), two),
                ],
            )
        ],
        after=(here_1f,),
    )
    intra_1 = across(intra)
    streams = [((0, two), stream_1f), (rest, stream_1n)]

    middle, near = (two, three), (three, rows)
    stream_2m, (inter,), _ = step(
        1, middle,
        streams[1:],
        [(everything, False, local_1n), ((two, 2 * two), False, inn_1f)],
        [("out", middle)],
        [],
    )
    inter_2m = cross(inter)
    stream_2n, (intra,), (local_2n, here_2m, inn_2m) = step(
        1, near,
        streams[1:],
        [(everything, False, local_1n), ((rows - two, rows), False, intra_1)],
        [("inn", near)],
        [(everything, [("here", near, 0), ("out", near, -three)])],
        late=[
            (
                middle, stream_2m,
                [(middle, [("here", middle, 0)]), ((two + three, rows), [("inn", middle, three)])],
            )
        ],
    )
    intra_2 = across(intra)
    stream_2f, (inter,), (here_2f, inn_2f) = step(
        1, (0, two),
        streams[:1],
        [
            (everything, False, local_1n),
            ((0, two), False, here_1f),
            ((0, two), True, inter_1),
        ],
        [("out", (0, two))],
        [((0, two), [("here", (0, two), 0)]), ((three, three + two), [("inn", (0, two), three)])],
        after=(local_2n,),
    )
    inter_2f = cross(inter)

    stream_3n, (inter, intra), (local_3n,) = step(
        2, near,
        [(near, stream_2n)],
        [
            (everything, False, local_2n),
            ((three, three + two), False, inn_2f),
            ((two + three, rows), False, inn_2m),
            (near, False, intra_2),
        ],
        [("out", near), ("inn", near)],
        [(near, [("here", near, 0)])],
    )
    inter_3n, intra_3n = cross(inter), across(intra)
    parts = [(0, tracks // 2), (tracks // 2, tracks - tracks // 2)]
    ends, after = [], (local_3n,)
    for first, part in parts:
        stream_3f, (inter, intra), (local_3f,) = step(
            2, (0, three),
            [((0, two), stream_2f), (middle, stream_2m)],
            [
                (everything, False, local_2n),
                ((0, two), False, here_2f),
                (middle, False, here_2m),
                ((0, two), True, inter_2m),
                (middle, True, inter_2f),
            ],
            [("out", (0, three)), ("inn", (0, three))],
            [((0, three), [("here", (0, three), 0)])],
            after=after, first=first, part=part,
        )
        after = (local_3f,)
        ends.append((stream_3f, local_3f, cross(inter), across(intra)))

    far_ends, near_ends = [], []
    for (first, part), (stream_3f, local_3f, inter, intra) in zip(parts, ends):
        far_ends.append(
            ((0, three), first, part, (0, 0, first, first), (stream_3f, local_3f, intra_3n, inter_3n))
        )
        near_ends.append(
            (near, first, part, (first, first, 0, 0), (stream_3n, local_3n, intra, inter))
        )
    out = []
    for q, first, part, bases, arrays in far_ends + near_ends:
        count = q[1] - q[0]
        out = [
            pl.pallas_call(
                functools.partial(last_kernel, blocks - 1, q, rows, first, bases),
                in_specs=[vmem] * 7 + [hbm] * len(out),
                out_specs=hbm,
                out_shape=jax.ShapeDtypeStruct(tower_in.shape, jnp.bfloat16),
                scratch_shapes=[
                    pltpu.VMEM((part, count, channels), jnp.bfloat16),
                    pltpu.SemaphoreType.DMA((part,)),
                ],
                input_output_aliases={7: 0} if out else {},
                compiler_params=params,
                cost_estimate=cost(count, conv=0, part=part),
            )(*arrays, *mids, *out)
        ]
    return out[0]


def solution(mesh):
    placed = (P("groups", "seq", None), P(), P(), P(), P(), P(), P())
    return jax.shard_map(
        local, mesh=mesh, in_specs=placed, out_specs=P("groups", "seq", None), check_vma=False
    )
```

```python
import functools

import jax
import jax.numpy as jnp
from jax import lax
from jax.experimental import pallas as pl
from jax.experimental.pallas import tpu as pltpu
from jax.sharding import PartitionSpec as P

FIRST_DILATION = 32
MIB = 1024 * 1024
TAPS = 3


def place():
    index = lax.axis_index("seq")
    even = lax.rem(index, 2) == 0
    edge = jnp.logical_or(index == 0, index == lax.axis_size("seq") - 1)
    return even, edge


def both_ways(body):
    even, edge = place()
    pl.when(even)(lambda: body(True, edge))
    pl.when(jnp.logical_not(even))(lambda: body(False, edge))


def span_of(q, within, even):
    if even:
        return slice(q[0] - within[0], q[1] - within[0])
    return slice(within[1] - q[1], within[1] - q[0])


def value_term(value, within, even):
    return within, lambda q: value[span_of(q, within, even)]


def ref_term(ref, t, within, even, drop=None):
    def get(q):
        part = ref[t, span_of(q, within, even)].astype(jnp.float32)
        return part if drop is None else jnp.where(drop, 0.0, part)

    return within, get


def assemble(q, terms, even):
    cuts = sorted({q[0], q[1], *(min(max(c, q[0]), q[1]) for rows, _ in terms for c in rows)})
    pieces = []
    for low, high in zip(cuts[:-1], cuts[1:]):
        total = None
        for rows, get in terms:
            if rows[0] <= low and high <= rows[1]:
                part = get((low, high))
                total = part if total is None else total + part
        pieces.append(total)
    if not even:
        pieces = pieces[::-1]
    return pieces[0] if len(pieces) == 1 else jnp.concatenate(pieces, axis=0)


def moved(value, within, q, by, even):
    return (q[0] + by, q[1] + by), lambda to: value[
        span_of((to[0] - by, to[1] - by), within, even)
    ]


def normed_of(stream, scale, shift):
    return jnp.maximum(stream.astype(jnp.float32) * scale + shift, 0.0).astype(jnp.bfloat16)


def products_of(stream, block, even, names, scale_ref, shift_ref, weight_ref):
    filters = weight_ref.shape[-1]
    normed = normed_of(stream, scale_ref[block : block + 1], shift_ref[block : block + 1])
    order = ("inn", "here", "out") if even else ("out", "here", "inn")
    chosen = [(k, name) for k, name in enumerate(order) if name in names]
    weight = jnp.concatenate([weight_ref[block, k] for k, _ in chosen], axis=1)
    product = jnp.dot(normed, weight, preferred_element_type=jnp.float32)
    return {
        name: product[:, i * filters : (i + 1) * filters] for i, (_, name) in enumerate(chosen)
    }


def finished(stream, conv, block, scale_ref, shift_ref, point_ref):
    middle = jnp.maximum(
        conv * scale_ref[block : block + 1] + shift_ref[block : block + 1], 0.0
    ).astype(jnp.bfloat16)
    update = jnp.dot(middle, point_ref[block], preferred_element_type=jnp.float32)
    return (stream.astype(jnp.float32) + update).astype(jnp.bfloat16)


def stacked(parts):
    return jnp.concatenate(parts, axis=0)


def edge_kernel(
    span, tower_ref, scale_ref, shift_ref, weight_ref, inter_ref, part, scale, shift, weight, sems
):
    tracks, rows, channels = tower_ref.shape

    def body(even, edge):
        source = tower_ref.at[:, span_of((0, span), (0, rows), even)]
        copies = [
            pltpu.make_async_copy(source, target, sems.at[i])
            for i, (source, target) in enumerate(
                [
                    (source, part),
                    (weight_ref.at[0, TAPS - 1 if even else 0], weight),
                    (scale_ref, scale),
                    (shift_ref, shift),
                ]
            )
        ]
        for copy in copies:
            copy.start()
        for i in (2, 3, 0):
            copies[i].wait()
        normed = normed_of(part[...].reshape(tracks * span, channels), scale[0:1], shift[0:1])
        copies[1].wait()
        inter_ref[...] = (
            jnp.dot(normed, weight[...], preferred_element_type=jnp.float32)
            .astype(jnp.bfloat16)
            .reshape(inter_ref.shape)
        )

    both_ways(body)


def entry_kernel(span, tower_ref, scale_ref, shift_ref, weight_ref, local_ref, intra_ref):
    tracks, rows, channels = tower_ref.shape
    everything = (0, rows)

    def body(even, edge):
        named = products_of(
            tower_ref[...].reshape(tracks * rows, channels),
            0, even, ("out", "here", "inn"), scale_ref, shift_ref, weight_ref,
        )
        out, here, inn = named["out"], named["here"], named["inn"]
        for t in range(tracks):
            own = slice(t * rows, (t + 1) * rows)
            intra_ref[t] = inn[own][span_of((rows - span, rows), everything, even)].astype(
                jnp.bfloat16
            )
            local_ref[t] = assemble(
                everything,
                [
                    value_term(here[own], everything, even),
                    moved(out[own], everything, (span, rows), -span, even),
                    moved(inn[own], everything, (0, rows - span), span, even),
                ],
                even,
            )

    both_ways(body)


def step_kernel(plan, *refs):
    block, q, first, streams, terms, sends, keep, late = plan
    refs = list(refs)
    take = lambda n: [refs.pop(0) for _ in range(n)]
    stream_refs, term_refs, late_refs = take(len(streams)), take(len(terms)), take(len(late))
    mid_scale_ref, mid_shift_ref, point_ref = take(3)
    scale_ref, shift_ref, weight_ref = take(3)
    refs = refs[-(1 + len(sends) + len(keep) + sum(len(kept) for _, kept in late)) :]
    out_ref = refs.pop(0)
    send_refs, keep_refs = take(len(sends)), take(len(keep))
    late_keep_refs = [take(len(kept)) for _, kept in late]
    tracks, count = out_ref.shape[0], q[1] - q[0]

    def body(even, edge):
        conv = stacked(
            [
                assemble(
                    q,
                    [
                        ref_term(ref, first + t, rows, even, edge if crossed else None)
                        for ref, (rows, crossed) in zip(term_refs, terms)
                    ],
                    even,
                )
                for t in range(tracks)
            ]
        )
        stream = stacked(
            [
                assemble_stream(q, stream_refs, streams, first + t, even)
                for t in range(tracks)
            ]
        )
        stream = finished(stream, conv, block, mid_scale_ref, mid_shift_ref, point_ref)
        out_ref[...] = stream.reshape(out_ref.shape)
        names = {name for name, _ in sends} | {name for _, parts in keep for name, _, _ in parts}
        named = products_of(stream, block + 1, even, names, scale_ref, shift_ref, weight_ref)
        for t in range(tracks):
            own = slice(t * count, (t + 1) * count)
            for ref, (name, rows) in zip(send_refs, sends):
                ref[t] = named[name][own][span_of(rows, q, even)].astype(jnp.bfloat16)
        store(named, q, keep_refs, keep, even)
        for ref, kept_refs, (rows, kept) in zip(late_refs, late_keep_refs, late):
            stream = ref[...].reshape(-1, ref.shape[-1])
            names = {name for _, parts in kept for name, _, _ in parts}
            named = products_of(stream, block + 1, even, names, scale_ref, shift_ref, weight_ref)
            store(named, rows, kept_refs, kept, even)

    def store(named, q, keep_refs, keep, even):
        count = q[1] - q[0]
        for t in range(tracks):
            own = slice(t * count, (t + 1) * count)
            for ref, (rows, parts) in zip(keep_refs, keep):
                ref[t] = assemble(
                    rows,
                    [moved(named[name][own], q, part, by, even) for name, part, by in parts],
                    even,
                )

    both_ways(body)


def assemble_stream(q, stream_refs, streams, t, even):
    pieces = []
    for ref, within in zip(stream_refs, streams):
        low, high = max(q[0], within[0]), min(q[1], within[1])
        if low < high:
            pieces.append(ref[t, span_of((low, high), within, even)])
    if not even:
        pieces = pieces[::-1]
    return pieces[0] if len(pieces) == 1 else jnp.concatenate(pieces, axis=0)


def last_kernel(
    block, q, rows, first, bases, stream_ref, local_ref, intra_ref, inter_ref, *refs
):
    mid_scale_ref, mid_shift_ref, point_ref = refs[:3]
    out_ref, result, sems = refs[-3:]

    def body(even, edge):
        target = span_of(q, (0, rows), even)
        copies = []
        for t in range(result.shape[0]):
            stream, local, intra, inter = (
                ref[base + t]
                for ref, base in zip((stream_ref, local_ref, intra_ref, inter_ref), bases)
            )
            conv = (
                local
                + intra.astype(jnp.float32)
                + jnp.where(edge, 0.0, inter.astype(jnp.float32))
            )
            result[t] = finished(stream, conv, block, mid_scale_ref, mid_shift_ref, point_ref)
            copies.append(
                pltpu.make_async_copy(result.at[t], out_ref.at[first + t, target], sems.at[t])
            )
            copies[-1].start()
        for copy in copies:
            copy.wait()

    both_ways(body)


def swaps(groups, devices):
    intra, inter = [], []
    for g in range(groups):
        base = g * devices
        intra += [(base + i, base + i + 1) for i in range(0, devices - 1, 2)]
        inter += [(base + i, base + i + 1) for i in range(1, devices - 1, 2)]
    for g in range(0, groups - 1, 2):
        for end in (0, devices - 1):
            inter.append((g * devices + end, (g + 1) * devices + end))
    return tuple(pairs + [(b, a) for a, b in pairs] for pairs in (intra, inter))


def local(
    tower_in, first_norm_scale, first_norm_shift, conv_weight, mid_scale, second_norm_shift, point_weight
):
    tracks, rows, channels = tower_in.shape
    blocks, _, _, filters = conv_weight.shape
    intra_pairs, inter_pairs = swaps(lax.axis_size("groups"), lax.axis_size("seq"))
    spans = [FIRST_DILATION * 2**b for b in range(blocks)]
    vmem = pl.BlockSpec(memory_space=pltpu.VMEM)
    hbm = pl.BlockSpec(memory_space=pltpu.HBM)
    params = pltpu.CompilerParams(vmem_limit_bytes=32 * MIB)
    norms = (first_norm_scale, first_norm_shift)
    mids = (mid_scale, second_norm_shift, point_weight)

    def cross(value):
        return lax.ppermute(value, ("groups", "seq"), inter_pairs)

    def across(value):
        return lax.ppermute(value, ("groups", "seq"), intra_pairs)

    def cost(count, conv=1, point=1, part=tracks):
        flops = 20 * part * count * channels * filters * (TAPS * conv + point)
        return pl.CostEstimate(flops=flops, bytes_accessed=flops // 1000, transcendentals=0)

    def halo(count, part=tracks):
        return jax.ShapeDtypeStruct((part, count, filters), jnp.bfloat16)

    def sums(count, part=tracks):
        return jax.ShapeDtypeStruct((part, count, filters), jnp.float32)

    def step(block, q, streams, terms, sends, keep, after=(), first=0, part=tracks, late=()):
        plan = (
            block, q, first,
            [r for r, _ in streams], [(r, c) for r, c, _ in terms], sends, keep,
            [(r, kept) for r, _, kept in late],
        )
        arrays = [a for _, a in streams] + [a for _, _, a in terms] + [a for _, a, _ in late]
        kept_rows = [r for r, _ in keep] + [r for _, _, kept in late for r, _ in kept]
        count = q[1] - q[0]
        made = pl.pallas_call(
            functools.partial(step_kernel, plan),
            in_specs=[vmem] * (len(arrays) + 6 + len(after)),
            out_specs=[vmem] * (1 + len(sends) + len(kept_rows)),
            out_shape=[jax.ShapeDtypeStruct((part, count, channels), jnp.bfloat16)]
            + [halo(r[1] - r[0], part) for _, r in sends]
            + [sums(r[1] - r[0], part) for r in kept_rows],
            compiler_params=params,
            cost_estimate=cost(count, part=part),
        )(*arrays, *mids, *norms, conv_weight, *after)
        return made[0], made[1 : 1 + len(sends)], made[1 + len(sends) :]

    everything = (0, rows)
    one, two, three, four = spans

    far = [
        pltpu.with_memory_space_constraint(x, pltpu.HBM)
        for x in (tower_in, first_norm_scale, first_norm_shift, conv_weight)
    ]
    inter = pl.pallas_call(
        functools.partial(edge_kernel, one),
        in_specs=[hbm] * 4,
        out_specs=vmem,
        out_shape=halo(one),
        scratch_shapes=[pltpu.VMEM((tracks, one, channels), jnp.bfloat16)]
        + [pltpu.VMEM(first_norm_scale.shape, jnp.float32)] * 2
        + [pltpu.VMEM((channels, filters), jnp.bfloat16), pltpu.SemaphoreType.DMA((4,))],
        compiler_params=params,
        cost_estimate=cost(one, point=0),
    )(*far)
    inter_0 = cross(inter)
    local_0, intra = pl.pallas_call(
        functools.partial(entry_kernel, one),
        in_specs=[vmem] * 4,
        out_specs=[vmem] * 2,
        out_shape=[sums(rows), halo(one)],
        compiler_params=params,
        cost_estimate=cost(rows, point=0),
    )(tower_in, *norms, conv_weight)
    intra_0 = across(intra)

    edges, middle, inner, ends = (0, two), (two, three), (three, rows - two), (rows - two, rows)
    near = (three, rows)
    stream_1p, _, (local_1p,) = step(
        0, inner,
        [(everything, tower_in)],
        [(everything, False, local_0)],
        [],
        [((two, rows), [("here", inner, 0), ("out", inner, -two), ("inn", inner, two)])],
    )
    stream_1f, (inter,), (here_1f, inn_1f) = step(
        0, edges,
        [(everything, tower_in)],
        [(everything, False, local_0), ((0, one), True, inter_0)],
        [("out", edges)],
        [(edges, [("here", edges, 0)]), (middle, [("inn", edges, two)])],
        after=(local_1p,),
    )
    inter_1 = cross(inter)
    stream_1m, _, (local_1m,) = step(
        0, middle,
        [(everything, tower_in)],
        [(everything, False, local_0)],
        [],
        [((0, rows - two), [("here", middle, 0), ("out", middle, -two), ("inn", middle, two)])],
        after=(here_1f,),
    )
    stream_1e, (intra,), (local_1e,) = step(
        0, ends,
        [(everything, tower_in)],
        [(everything, False, local_0), ((rows - one, rows), False, intra_0)],
        [("inn", ends)],
        [((three, rows), [("here", ends, 0), ("out", ends, -two)])],
        after=(local_1m,),
    )
    intra_1 = across(intra)

    stream_2m, (inter,), _ = step(
        1, middle,
        [(middle, stream_1m)],
        [
            ((two, rows), False, local_1p),
            ((0, rows - two), False, local_1m),
            (middle, False, inn_1f),
        ],
        [("out", middle)],
        [],
        after=(local_1e,),
    )
    inter_2m = cross(inter)
    stream_2n, (intra,), (local_2n, here_2m, inn_2m) = step(
        1, near,
        [(inner, stream_1p), (ends, stream_1e)],
        [
            ((two, rows), False, local_1p),
            ((0, rows - two), False, local_1m),
            (near, False, local_1e),
            (ends, False, intra_1),
        ],
        [("inn", near)],
        [(everything, [("here", near, 0), ("out", near, -three)])],
        late=[
            (
                middle, stream_2m,
                [(middle, [("here", middle, 0)]), ((two + three, rows), [("inn", middle, three)])],
            )
        ],
    )
    intra_2 = across(intra)
    stream_2f, (inter,), (here_2f, inn_2f) = step(
        1, edges,
        [(edges, stream_1f)],
        [
            ((0, rows - two), False, local_1m),
            (edges, False, here_1f),
            (edges, True, inter_1),
        ],
        [("out", edges)],
        [(edges, [("here", edges, 0)]), ((three, three + two), [("inn", edges, three)])],
        after=(local_2n,),
    )
    inter_2f = cross(inter)

    stream_3n, (inter, intra), (local_3n,) = step(
        2, near,
        [(near, stream_2n)],
        [
            (everything, False, local_2n),
            ((three, three + two), False, inn_2f),
            ((two + three, rows), False, inn_2m),
            (near, False, intra_2),
        ],
        [("out", near), ("inn", near)],
        [(near, [("here", near, 0)])],
    )
    inter_3n, intra_3n = cross(inter), across(intra)
    parts = [(0, tracks // 2), (tracks // 2, tracks - tracks // 2)]
    last, after = [], (local_3n,)
    for first, part in parts:
        stream_3f, (inter, intra), (local_3f,) = step(
            2, (0, three),
            [((0, two), stream_2f), (middle, stream_2m)],
            [
                (everything, False, local_2n),
                ((0, two), False, here_2f),
                (middle, False, here_2m),
                ((0, two), True, inter_2m),
                (middle, True, inter_2f),
            ],
            [("out", (0, three)), ("inn", (0, three))],
            [((0, three), [("here", (0, three), 0)])],
            after=after, first=first, part=part,
        )
        after = (local_3f,)
        last.append((stream_3f, local_3f, cross(inter), across(intra)))

    far_ends, near_ends = [], []
    for (first, part), (stream_3f, local_3f, inter, intra) in zip(parts, last):
        far_ends.append(
            ((0, three), first, part, (0, 0, first, first), (stream_3f, local_3f, intra_3n, inter_3n))
        )
        near_ends.append(
            (near, first, part, (first, first, 0, 0), (stream_3n, local_3n, intra, inter))
        )
    out = []
    for q, first, part, bases, arrays in far_ends + near_ends:
        count = q[1] - q[0]
        out = [
            pl.pallas_call(
                functools.partial(last_kernel, blocks - 1, q, rows, first, bases),
                in_specs=[vmem] * 7 + [hbm] * len(out),
                out_specs=hbm,
                out_shape=jax.ShapeDtypeStruct(tower_in.shape, jnp.bfloat16),
                scratch_shapes=[
                    pltpu.VMEM((part, count, channels), jnp.bfloat16),
                    pltpu.SemaphoreType.DMA((part,)),
                ],
                input_output_aliases={7: 0} if out else {},
                compiler_params=params,
                cost_estimate=cost(count, conv=0, part=part),
            )(*arrays, *mids, *out)
        ]
    return out[0]


def solution(mesh):
    placed = (P("groups", "seq", None), P(), P(), P(), P(), P(), P())
    return jax.shard_map(
        local, mesh=mesh, in_specs=placed, out_specs=P("groups", "seq", None), check_vma=False
    )
```

```python
import functools

import jax
import jax.numpy as jnp
from jax import lax
from jax.experimental import pallas as pl
from jax.experimental.pallas import tpu as pltpu
from jax.sharding import PartitionSpec as P

FIRST_DILATION = 32
MIB = 1024 * 1024
TAPS = 3


def place():
    index = lax.axis_index("seq")
    even = lax.rem(index, 2) == 0
    edge = jnp.logical_or(index == 0, index == lax.axis_size("seq") - 1)
    return even, edge


def both_ways(body):
    even, edge = place()
    pl.when(even)(lambda: body(True, edge))
    pl.when(jnp.logical_not(even))(lambda: body(False, edge))


def span_of(q, within, even):
    if even:
        return slice(q[0] - within[0], q[1] - within[0])
    return slice(within[1] - q[1], within[1] - q[0])


def value_term(value, within, even):
    return within, lambda q: value[span_of(q, within, even)]


def ref_term(ref, t, within, even, drop=None):
    def get(q):
        part = ref[t, span_of(q, within, even)].astype(jnp.float32)
        return part if drop is None else jnp.where(drop, 0.0, part)

    return within, get


def assemble(q, terms, even):
    cuts = sorted({q[0], q[1], *(min(max(c, q[0]), q[1]) for rows, _ in terms for c in rows)})
    pieces = []
    for low, high in zip(cuts[:-1], cuts[1:]):
        total = None
        for rows, get in terms:
            if rows[0] <= low and high <= rows[1]:
                part = get((low, high))
                total = part if total is None else total + part
        pieces.append(total)
    if not even:
        pieces = pieces[::-1]
    return pieces[0] if len(pieces) == 1 else jnp.concatenate(pieces, axis=0)


def moved(value, within, q, by, even):
    return (q[0] + by, q[1] + by), lambda to: value[
        span_of((to[0] - by, to[1] - by), within, even)
    ]


def normed_of(stream, scale, shift):
    return jnp.maximum(stream.astype(jnp.float32) * scale + shift, 0.0).astype(jnp.bfloat16)


def products_of(stream, block, even, names, scale_ref, shift_ref, weight_ref):
    filters = weight_ref.shape[-1]
    normed = normed_of(stream, scale_ref[block : block + 1], shift_ref[block : block + 1])
    order = ("inn", "here", "out") if even else ("out", "here", "inn")
    chosen = [(k, name) for k, name in enumerate(order) if name in names]
    weight = jnp.concatenate([weight_ref[block, k] for k, _ in chosen], axis=1)
    product = jnp.dot(normed, weight, preferred_element_type=jnp.float32)
    return {
        name: product[:, i * filters : (i + 1) * filters] for i, (_, name) in enumerate(chosen)
    }


def finished(stream, conv, block, scale_ref, shift_ref, point_ref):
    middle = jnp.maximum(
        conv * scale_ref[block : block + 1] + shift_ref[block : block + 1], 0.0
    ).astype(jnp.bfloat16)
    update = jnp.dot(middle, point_ref[block], preferred_element_type=jnp.float32)
    return (stream.astype(jnp.float32) + update).astype(jnp.bfloat16)


def stacked(parts):
    return jnp.concatenate(parts, axis=0)


def edge_kernel(
    span, tower_ref, scale_ref, shift_ref, weight_ref, inter_ref, part, scale, shift, weight, sems
):
    tracks, rows, channels = tower_ref.shape

    def body(even, edge):
        source = tower_ref.at[:, span_of((0, span), (0, rows), even)]
        copies = [
            pltpu.make_async_copy(source, target, sems.at[i])
            for i, (source, target) in enumerate(
                [
                    (source, part),
                    (weight_ref.at[0, TAPS - 1 if even else 0], weight),
                    (scale_ref, scale),
                    (shift_ref, shift),
                ]
            )
        ]
        for copy in copies:
            copy.start()
        for i in (2, 3, 0):
            copies[i].wait()
        normed = normed_of(part[...].reshape(tracks * span, channels), scale[0:1], shift[0:1])
        copies[1].wait()
        inter_ref[...] = (
            jnp.dot(normed, weight[...], preferred_element_type=jnp.float32)
            .astype(jnp.bfloat16)
            .reshape(inter_ref.shape)
        )

    both_ways(body)


def entry_kernel(span, tower_ref, scale_ref, shift_ref, weight_ref, local_ref, intra_ref):
    tracks, rows, channels = tower_ref.shape
    everything = (0, rows)

    def body(even, edge):
        named = products_of(
            tower_ref[...].reshape(tracks * rows, channels),
            0, even, ("out", "here", "inn"), scale_ref, shift_ref, weight_ref,
        )
        out, here, inn = named["out"], named["here"], named["inn"]
        for t in range(tracks):
            own = slice(t * rows, (t + 1) * rows)
            intra_ref[t] = inn[own][span_of((rows - span, rows), everything, even)].astype(
                jnp.bfloat16
            )
            local_ref[t] = assemble(
                everything,
                [
                    value_term(here[own], everything, even),
                    moved(out[own], everything, (span, rows), -span, even),
                    moved(inn[own], everything, (0, rows - span), span, even),
                ],
                even,
            )

    both_ways(body)


def step_kernel(plan, *refs):
    block, q, first, streams, terms, sends, keep, late = plan
    refs = list(refs)
    take = lambda n: [refs.pop(0) for _ in range(n)]
    stream_refs, term_refs, late_refs = take(len(streams)), take(len(terms)), take(len(late))
    mid_scale_ref, mid_shift_ref, point_ref = take(3)
    scale_ref, shift_ref, weight_ref = take(3)
    refs = refs[-(1 + len(sends) + len(keep) + sum(len(kept) for _, kept in late)) :]
    out_ref = refs.pop(0)
    send_refs, keep_refs = take(len(sends)), take(len(keep))
    late_keep_refs = [take(len(kept)) for _, kept in late]
    tracks, count = out_ref.shape[0], q[1] - q[0]

    def body(even, edge):
        conv = stacked(
            [
                assemble(
                    q,
                    [
                        ref_term(ref, first + t, rows, even, edge if crossed else None)
                        for ref, (rows, crossed) in zip(term_refs, terms)
                    ],
                    even,
                )
                for t in range(tracks)
            ]
        )
        stream = stacked(
            [
                assemble_stream(q, stream_refs, streams, first + t, even)
                for t in range(tracks)
            ]
        )
        stream = finished(stream, conv, block, mid_scale_ref, mid_shift_ref, point_ref)
        out_ref[...] = stream.reshape(out_ref.shape)
        names = {name for name, _ in sends} | {name for _, parts in keep for name, _, _ in parts}
        named = products_of(stream, block + 1, even, names, scale_ref, shift_ref, weight_ref)
        for t in range(tracks):
            own = slice(t * count, (t + 1) * count)
            for ref, (name, rows) in zip(send_refs, sends):
                ref[t] = named[name][own][span_of(rows, q, even)].astype(jnp.bfloat16)
        store(named, q, keep_refs, keep, even)
        for ref, kept_refs, (rows, kept) in zip(late_refs, late_keep_refs, late):
            stream = ref[...].reshape(-1, ref.shape[-1])
            names = {name for _, parts in kept for name, _, _ in parts}
            named = products_of(stream, block + 1, even, names, scale_ref, shift_ref, weight_ref)
            store(named, rows, kept_refs, kept, even)

    def store(named, q, keep_refs, keep, even):
        count = q[1] - q[0]
        for t in range(tracks):
            own = slice(t * count, (t + 1) * count)
            for ref, (rows, parts) in zip(keep_refs, keep):
                ref[t] = assemble(
                    rows,
                    [moved(named[name][own], q, part, by, even) for name, part, by in parts],
                    even,
                )

    both_ways(body)


def assemble_stream(q, stream_refs, streams, t, even):
    pieces = []
    for ref, within in zip(stream_refs, streams):
        low, high = max(q[0], within[0]), min(q[1], within[1])
        if low < high:
            pieces.append(ref[t, span_of((low, high), within, even)])
    if not even:
        pieces = pieces[::-1]
    return pieces[0] if len(pieces) == 1 else jnp.concatenate(pieces, axis=0)


def last_kernel(
    block, q, rows, first, bases, stream_ref, local_ref, intra_ref, inter_ref, *refs
):
    mid_scale_ref, mid_shift_ref, point_ref = refs[:3]
    out_ref, result, sems = refs[-3:]

    def body(even, edge):
        target = span_of(q, (0, rows), even)
        copies = []
        for t in range(result.shape[0]):
            stream, local, intra, inter = (
                ref[base + t]
                for ref, base in zip((stream_ref, local_ref, intra_ref, inter_ref), bases)
            )
            conv = (
                local
                + intra.astype(jnp.float32)
                + jnp.where(edge, 0.0, inter.astype(jnp.float32))
            )
            result[t] = finished(stream, conv, block, mid_scale_ref, mid_shift_ref, point_ref)
            copies.append(
                pltpu.make_async_copy(result.at[t], out_ref.at[first + t, target], sems.at[t])
            )
            copies[-1].start()
        for copy in copies:
            copy.wait()

    both_ways(body)


def swaps(groups, devices):
    intra, inter = [], []
    for g in range(groups):
        base = g * devices
        intra += [(base + i, base + i + 1) for i in range(0, devices - 1, 2)]
        inter += [(base + i, base + i + 1) for i in range(1, devices - 1, 2)]
    for g in range(0, groups - 1, 2):
        for end in (0, devices - 1):
            inter.append((g * devices + end, (g + 1) * devices + end))
    return tuple(pairs + [(b, a) for a, b in pairs] for pairs in (intra, inter))


def local(
    tower_in, first_norm_scale, first_norm_shift, conv_weight, mid_scale, second_norm_shift, point_weight
):
    tracks, rows, channels = tower_in.shape
    blocks, _, _, filters = conv_weight.shape
    intra_pairs, inter_pairs = swaps(lax.axis_size("groups"), lax.axis_size("seq"))
    spans = [FIRST_DILATION * 2**b for b in range(blocks)]
    vmem = pl.BlockSpec(memory_space=pltpu.VMEM)
    hbm = pl.BlockSpec(memory_space=pltpu.HBM)
    params = pltpu.CompilerParams(vmem_limit_bytes=32 * MIB)
    norms = (first_norm_scale, first_norm_shift)
    mids = (mid_scale, second_norm_shift, point_weight)

    def cross(value):
        return lax.ppermute(value, ("groups", "seq"), inter_pairs)

    def across(value):
        return lax.ppermute(value, ("groups", "seq"), intra_pairs)

    def cost(count, conv=1, point=1, part=tracks):
        flops = 20 * part * count * channels * filters * (TAPS * conv + point)
        return pl.CostEstimate(flops=flops, bytes_accessed=flops // 1000, transcendentals=0)

    def halo(count, part=tracks):
        return jax.ShapeDtypeStruct((part, count, filters), jnp.bfloat16)

    def sums(count, part=tracks):
        return jax.ShapeDtypeStruct((part, count, filters), jnp.float32)

    def step(block, q, streams, terms, sends, keep, after=(), first=0, part=tracks, late=()):
        plan = (
            block, q, first,
            [r for r, _ in streams], [(r, c) for r, c, _ in terms], sends, keep,
            [(r, kept) for r, _, kept in late],
        )
        arrays = [a for _, a in streams] + [a for _, _, a in terms] + [a for _, a, _ in late]
        kept_rows = [r for r, _ in keep] + [r for _, _, kept in late for r, _ in kept]
        count = q[1] - q[0]
        made = pl.pallas_call(
            functools.partial(step_kernel, plan),
            in_specs=[vmem] * (len(arrays) + 6 + len(after)),
            out_specs=[vmem] * (1 + len(sends) + len(kept_rows)),
            out_shape=[jax.ShapeDtypeStruct((part, count, channels), jnp.bfloat16)]
            + [halo(r[1] - r[0], part) for _, r in sends]
            + [sums(r[1] - r[0], part) for r in kept_rows],
            compiler_params=params,
            cost_estimate=cost(count, part=part),
        )(*arrays, *mids, *norms, conv_weight, *after)
        return made[0], made[1 : 1 + len(sends)], made[1 + len(sends) :]

    everything = (0, rows)
    one, two, three, four = spans

    far = [
        pltpu.with_memory_space_constraint(x, pltpu.HBM)
        for x in (tower_in, first_norm_scale, first_norm_shift, conv_weight)
    ]
    inter = pl.pallas_call(
        functools.partial(edge_kernel, one),
        in_specs=[hbm] * 4,
        out_specs=vmem,
        out_shape=halo(one),
        scratch_shapes=[pltpu.VMEM((tracks, one, channels), jnp.bfloat16)]
        + [pltpu.VMEM(first_norm_scale.shape, jnp.float32)] * 2
        + [pltpu.VMEM((channels, filters), jnp.bfloat16), pltpu.SemaphoreType.DMA((4,))],
        compiler_params=params,
        cost_estimate=cost(one, point=0),
    )(*far)
    inter_0 = cross(inter)
    local_0, intra = pl.pallas_call(
        functools.partial(entry_kernel, one),
        in_specs=[vmem] * 4,
        out_specs=[vmem] * 2,
        out_shape=[sums(rows), halo(one)],
        compiler_params=params,
        cost_estimate=cost(rows, point=0),
    )(tower_in, *norms, conv_weight)
    intra_0 = across(intra)

    edges, middle, inner, ends = (0, two), (two, three), (three, rows - two), (rows - two, rows)
    near = (three, rows)
    stream_1p, _, (local_1p,) = step(
        0, inner,
        [(everything, tower_in)],
        [(everything, False, local_0)],
        [],
        [((two, rows), [("here", inner, 0), ("out", inner, -two), ("inn", inner, two)])],
    )
    stream_1f, (inter,), (here_1f, inn_1f) = step(
        0, edges,
        [(everything, tower_in)],
        [(everything, False, local_0), ((0, one), True, inter_0)],
        [("out", edges)],
        [(edges, [("here", edges, 0)]), (middle, [("inn", edges, two)])],
        after=(local_1p,),
    )
    inter_1 = cross(inter)
    stream_1m, _, (local_1m,) = step(
        0, middle,
        [(everything, tower_in)],
        [(everything, False, local_0)],
        [],
        [((0, rows - two), [("here", middle, 0), ("out", middle, -two), ("inn", middle, two)])],
        after=(here_1f,),
    )
    stream_1e, (intra,), (local_1e,) = step(
        0, ends,
        [(everything, tower_in)],
        [(everything, False, local_0), ((rows - one, rows), False, intra_0)],
        [("inn", ends)],
        [((three, rows), [("here", ends, 0), ("out", ends, -two)])],
        after=(local_1m,),
    )
    intra_1 = across(intra)

    stream_2m, (inter,), _ = step(
        1, middle,
        [(middle, stream_1m)],
        [
            ((two, rows), False, local_1p),
            ((0, rows - two), False, local_1m),
            (middle, False, inn_1f),
        ],
        [("out", middle)],
        [],
        after=(local_1e,),
    )
    inter_2m = cross(inter)
    stream_2n, (intra,), (local_2n, here_2m, inn_2m) = step(
        1, near,
        [(inner, stream_1p), (ends, stream_1e)],
        [
            ((two, rows), False, local_1p),
            ((0, rows - two), False, local_1m),
            (near, False, local_1e),
            (ends, False, intra_1),
        ],
        [("inn", near)],
        [(everything, [("here", near, 0), ("out", near, -three)])],
        late=[
            (
                middle, stream_2m,
                [(middle, [("here", middle, 0)]), ((two + three, rows), [("inn", middle, three)])],
            )
        ],
    )
    intra_2 = across(intra)
    stream_2f, (inter,), (here_2f, inn_2f) = step(
        1, edges,
        [(edges, stream_1f)],
        [
            ((0, rows - two), False, local_1m),
            (edges, False, here_1f),
            (edges, True, inter_1),
        ],
        [("out", edges)],
        [(edges, [("here", edges, 0)]), ((three, three + two), [("inn", edges, three)])],
        after=(local_2n,),
    )
    inter_2f = cross(inter)

    stream_3n, (inter, intra), (local_3n,) = step(
        2, near,
        [(near, stream_2n)],
        [
            (everything, False, local_2n),
            ((three, three + two), False, inn_2f),
            ((two + three, rows), False, inn_2m),
            (near, False, intra_2),
        ],
        [("out", near), ("inn", near)],
        [(near, [("here", near, 0)])],
    )
    inter_3n, kept_3n = cross(inter), intra
    parts = [(0, tracks // 2), (tracks // 2, tracks - tracks // 2)]
    last, after = [], (local_3n,)
    for first, part in parts:
        stream_3f, (inter, intra), (local_3f,) = step(
            2, (0, three),
            [((0, two), stream_2f), (middle, stream_2m)],
            [
                (everything, False, local_2n),
                ((0, two), False, here_2f),
                (middle, False, here_2m),
                ((0, two), True, inter_2m),
                (middle, True, inter_2f),
            ],
            [("out", (0, three)), ("inn", (0, three))],
            [((0, three), [("here", (0, three), 0)])],
            after=after, first=first, part=part,
        )
        after = (local_3f,)
        if first == 0:
            kept_3n, intra = lax.optimization_barrier((kept_3n, intra))
            intra_3n = across(kept_3n)
        last.append((stream_3f, local_3f, cross(inter), across(intra)))

    far_ends, near_ends = [], []
    for (first, part), (stream_3f, local_3f, inter, intra) in zip(parts, last):
        far_ends.append(
            ((0, three), first, part, (0, 0, first, first), (stream_3f, local_3f, intra_3n, inter_3n))
        )
        near_ends.append(
            (near, first, part, (first, first, 0, 0), (stream_3n, local_3n, intra, inter))
        )
    out = []
    for q, first, part, bases, arrays in far_ends + near_ends:
        count = q[1] - q[0]
        out = [
            pl.pallas_call(
                functools.partial(last_kernel, blocks - 1, q, rows, first, bases),
                in_specs=[vmem] * 7 + [hbm] * len(out),
                out_specs=hbm,
                out_shape=jax.ShapeDtypeStruct(tower_in.shape, jnp.bfloat16),
                scratch_shapes=[
                    pltpu.VMEM((part, count, channels), jnp.bfloat16),
                    pltpu.SemaphoreType.DMA((part,)),
                ],
                input_output_aliases={7: 0} if out else {},
                compiler_params=params,
                cost_estimate=cost(count, conv=0, part=part),
            )(*arrays, *mids, *out)
        ]
    return out[0]


def solution(mesh):
    placed = (P("groups", "seq", None), P(), P(), P(), P(), P(), P())
    return jax.shard_map(
        local, mesh=mesh, in_specs=placed, out_specs=P("groups", "seq", None), check_vma=False
    )
```

```python
import functools

import jax
import jax.numpy as jnp
from jax import lax
from jax.experimental import pallas as pl
from jax.experimental.pallas import tpu as pltpu
from jax.sharding import PartitionSpec as P

FIRST_DILATION = 32
MIB = 1024 * 1024
TAPS = 3


def place():
    index = lax.axis_index("seq")
    even = lax.rem(index, 2) == 0
    edge = jnp.logical_or(index == 0, index == lax.axis_size("seq") - 1)
    return even, edge


def both_ways(body):
    even, edge = place()
    pl.when(even)(lambda: body(True, edge))
    pl.when(jnp.logical_not(even))(lambda: body(False, edge))


def span_of(q, within, even):
    if even:
        return slice(q[0] - within[0], q[1] - within[0])
    return slice(within[1] - q[1], within[1] - q[0])


def value_term(value, within, even):
    return within, lambda q: value[span_of(q, within, even)]


def ref_term(ref, t, within, even, drop=None):
    def get(q):
        part = ref[t, span_of(q, within, even)].astype(jnp.float32)
        return part if drop is None else jnp.where(drop, 0.0, part)

    return within, get


def assemble(q, terms, even):
    cuts = sorted({q[0], q[1], *(min(max(c, q[0]), q[1]) for rows, _ in terms for c in rows)})
    pieces = []
    for low, high in zip(cuts[:-1], cuts[1:]):
        total = None
        for rows, get in terms:
            if rows[0] <= low and high <= rows[1]:
                part = get((low, high))
                total = part if total is None else total + part
        pieces.append(total)
    if not even:
        pieces = pieces[::-1]
    return pieces[0] if len(pieces) == 1 else jnp.concatenate(pieces, axis=0)


def moved(value, within, q, by, even):
    return (q[0] + by, q[1] + by), lambda to: value[
        span_of((to[0] - by, to[1] - by), within, even)
    ]


def normed_of(stream, scale, shift):
    return jnp.maximum(stream.astype(jnp.float32) * scale + shift, 0.0).astype(jnp.bfloat16)


def products_of(stream, block, even, names, scale_ref, shift_ref, weight_ref):
    filters = weight_ref.shape[-1]
    normed = normed_of(stream, scale_ref[block : block + 1], shift_ref[block : block + 1])
    order = ("inn", "here", "out") if even else ("out", "here", "inn")
    chosen = [(k, name) for k, name in enumerate(order) if name in names]
    weight = jnp.concatenate([weight_ref[block, k] for k, _ in chosen], axis=1)
    product = jnp.dot(normed, weight, preferred_element_type=jnp.float32)
    return {
        name: product[:, i * filters : (i + 1) * filters] for i, (_, name) in enumerate(chosen)
    }


def finished(stream, conv, block, scale_ref, shift_ref, point_ref):
    middle = jnp.maximum(
        conv * scale_ref[block : block + 1] + shift_ref[block : block + 1], 0.0
    ).astype(jnp.bfloat16)
    update = jnp.dot(middle, point_ref[block], preferred_element_type=jnp.float32)
    return (stream.astype(jnp.float32) + update).astype(jnp.bfloat16)


def stacked(parts):
    return jnp.concatenate(parts, axis=0)


def edge_kernel(
    span, tower_ref, scale_ref, shift_ref, weight_ref, inter_ref, part, scale, shift, weight, sems
):
    tracks, rows, channels = tower_ref.shape

    def body(even, edge):
        source = tower_ref.at[:, span_of((0, span), (0, rows), even)]
        copies = [
            pltpu.make_async_copy(source, target, sems.at[i])
            for i, (source, target) in enumerate(
                [
                    (source, part),
                    (weight_ref.at[0, TAPS - 1 if even else 0], weight),
                    (scale_ref, scale),
                    (shift_ref, shift),
                ]
            )
        ]
        for copy in copies:
            copy.start()
        for i in (2, 3, 0):
            copies[i].wait()
        normed = normed_of(part[...].reshape(tracks * span, channels), scale[0:1], shift[0:1])
        copies[1].wait()
        inter_ref[...] = (
            jnp.dot(normed, weight[...], preferred_element_type=jnp.float32)
            .astype(jnp.bfloat16)
            .reshape(inter_ref.shape)
        )

    both_ways(body)


def entry_kernel(span, tower_ref, scale_ref, shift_ref, weight_ref, local_ref, intra_ref):
    tracks, rows, channels = tower_ref.shape
    everything = (0, rows)

    def body(even, edge):
        named = products_of(
            tower_ref[...].reshape(tracks * rows, channels),
            0, even, ("out", "here", "inn"), scale_ref, shift_ref, weight_ref,
        )
        out, here, inn = named["out"], named["here"], named["inn"]
        for t in range(tracks):
            own = slice(t * rows, (t + 1) * rows)
            intra_ref[t] = inn[own][span_of((rows - span, rows), everything, even)].astype(
                jnp.bfloat16
            )
            local_ref[t] = assemble(
                everything,
                [
                    value_term(here[own], everything, even),
                    moved(out[own], everything, (span, rows), -span, even),
                    moved(inn[own], everything, (0, rows - span), span, even),
                ],
                even,
            )

    both_ways(body)


def step_kernel(plan, *refs):
    block, q, first, streams, terms, sends, keep, late = plan
    refs = list(refs)
    take = lambda n: [refs.pop(0) for _ in range(n)]
    stream_refs, term_refs, late_refs = take(len(streams)), take(len(terms)), take(len(late))
    mid_scale_ref, mid_shift_ref, point_ref = take(3)
    scale_ref, shift_ref, weight_ref = take(3)
    refs = refs[-(1 + len(sends) + len(keep) + sum(len(kept) for _, kept in late)) :]
    out_ref = refs.pop(0)
    send_refs, keep_refs = take(len(sends)), take(len(keep))
    late_keep_refs = [take(len(kept)) for _, kept in late]
    tracks, count = out_ref.shape[0], q[1] - q[0]

    def body(even, edge):
        conv = stacked(
            [
                assemble(
                    q,
                    [
                        ref_term(ref, first + t, rows, even, edge if crossed else None)
                        for ref, (rows, crossed) in zip(term_refs, terms)
                    ],
                    even,
                )
                for t in range(tracks)
            ]
        )
        stream = stacked(
            [
                assemble_stream(q, stream_refs, streams, first + t, even)
                for t in range(tracks)
            ]
        )
        stream = finished(stream, conv, block, mid_scale_ref, mid_shift_ref, point_ref)
        out_ref[...] = stream.reshape(out_ref.shape)
        names = {name for name, _ in sends} | {name for _, parts in keep for name, _, _ in parts}
        named = products_of(stream, block + 1, even, names, scale_ref, shift_ref, weight_ref)
        for t in range(tracks):
            own = slice(t * count, (t + 1) * count)
            for ref, (name, rows) in zip(send_refs, sends):
                ref[t] = named[name][own][span_of(rows, q, even)].astype(jnp.bfloat16)
        store(named, q, keep_refs, keep, even)
        for ref, kept_refs, (rows, kept) in zip(late_refs, late_keep_refs, late):
            stream = ref[...].reshape(-1, ref.shape[-1])
            names = {name for _, parts in kept for name, _, _ in parts}
            named = products_of(stream, block + 1, even, names, scale_ref, shift_ref, weight_ref)
            store(named, rows, kept_refs, kept, even)

    def store(named, q, keep_refs, keep, even):
        count = q[1] - q[0]
        for t in range(tracks):
            own = slice(t * count, (t + 1) * count)
            for ref, (rows, parts) in zip(keep_refs, keep):
                ref[t] = assemble(
                    rows,
                    [moved(named[name][own], q, part, by, even) for name, part, by in parts],
                    even,
                )

    both_ways(body)


def assemble_stream(q, stream_refs, streams, t, even):
    pieces = []
    for ref, within in zip(stream_refs, streams):
        low, high = max(q[0], within[0]), min(q[1], within[1])
        if low < high:
            pieces.append(ref[t, span_of((low, high), within, even)])
    if not even:
        pieces = pieces[::-1]
    return pieces[0] if len(pieces) == 1 else jnp.concatenate(pieces, axis=0)


def last_kernel(block, q, rows, groups, *refs):
    count = 4 * len(groups)
    mid_scale_ref, mid_shift_ref, point_ref = refs[count : count + 3]
    out_ref, result, sems = refs[-3:]

    def body(even, edge):
        target = span_of(q, (0, rows), even)
        copies = []
        for i, (first, part, bases) in enumerate(groups):
            for t in range(part):
                stream, local, intra, inter = (
                    ref[base + t] for ref, base in zip(refs[4 * i : 4 * i + 4], bases)
                )
                conv = (
                    local
                    + intra.astype(jnp.float32)
                    + jnp.where(edge, 0.0, inter.astype(jnp.float32))
                )
                done = len(copies)
                result[done] = finished(
                    stream, conv, block, mid_scale_ref, mid_shift_ref, point_ref
                )
                copies.append(
                    pltpu.make_async_copy(
                        result.at[done], out_ref.at[first + t, target], sems.at[done]
                    )
                )
                copies[-1].start()
        for copy in copies:
            copy.wait()

    both_ways(body)


def swaps(groups, devices):
    intra, inter = [], []
    for g in range(groups):
        base = g * devices
        intra += [(base + i, base + i + 1) for i in range(0, devices - 1, 2)]
        inter += [(base + i, base + i + 1) for i in range(1, devices - 1, 2)]
    for g in range(0, groups - 1, 2):
        for end in (0, devices - 1):
            inter.append((g * devices + end, (g + 1) * devices + end))
    return tuple(pairs + [(b, a) for a, b in pairs] for pairs in (intra, inter))


def local(
    tower_in, first_norm_scale, first_norm_shift, conv_weight, mid_scale, second_norm_shift, point_weight
):
    tracks, rows, channels = tower_in.shape
    blocks, _, _, filters = conv_weight.shape
    intra_pairs, inter_pairs = swaps(lax.axis_size("groups"), lax.axis_size("seq"))
    spans = [FIRST_DILATION * 2**b for b in range(blocks)]
    vmem = pl.BlockSpec(memory_space=pltpu.VMEM)
    hbm = pl.BlockSpec(memory_space=pltpu.HBM)
    params = pltpu.CompilerParams(vmem_limit_bytes=32 * MIB)
    norms = (first_norm_scale, first_norm_shift)
    mids = (mid_scale, second_norm_shift, point_weight)

    def cross(value):
        return lax.ppermute(value, ("groups", "seq"), inter_pairs)

    def across(value):
        return lax.ppermute(value, ("groups", "seq"), intra_pairs)

    def cost(count, conv=1, point=1, part=tracks):
        flops = 20 * part * count * channels * filters * (TAPS * conv + point)
        return pl.CostEstimate(flops=flops, bytes_accessed=flops // 1000, transcendentals=0)

    def halo(count, part=tracks):
        return jax.ShapeDtypeStruct((part, count, filters), jnp.bfloat16)

    def sums(count, part=tracks):
        return jax.ShapeDtypeStruct((part, count, filters), jnp.float32)

    def step(block, q, streams, terms, sends, keep, after=(), first=0, part=tracks, late=()):
        plan = (
            block, q, first,
            [r for r, _ in streams], [(r, c) for r, c, _ in terms], sends, keep,
            [(r, kept) for r, _, kept in late],
        )
        arrays = [a for _, a in streams] + [a for _, _, a in terms] + [a for _, a, _ in late]
        kept_rows = [r for r, _ in keep] + [r for _, _, kept in late for r, _ in kept]
        count = q[1] - q[0]
        made = pl.pallas_call(
            functools.partial(step_kernel, plan),
            in_specs=[vmem] * (len(arrays) + 6 + len(after)),
            out_specs=[vmem] * (1 + len(sends) + len(kept_rows)),
            out_shape=[jax.ShapeDtypeStruct((part, count, channels), jnp.bfloat16)]
            + [halo(r[1] - r[0], part) for _, r in sends]
            + [sums(r[1] - r[0], part) for r in kept_rows],
            compiler_params=params,
            cost_estimate=cost(count, part=part),
        )(*arrays, *mids, *norms, conv_weight, *after)
        return made[0], made[1 : 1 + len(sends)], made[1 + len(sends) :]

    everything = (0, rows)
    one, two, three, four = spans

    far = [
        pltpu.with_memory_space_constraint(x, pltpu.HBM)
        for x in (tower_in, first_norm_scale, first_norm_shift, conv_weight)
    ]
    inter = pl.pallas_call(
        functools.partial(edge_kernel, one),
        in_specs=[hbm] * 4,
        out_specs=vmem,
        out_shape=halo(one),
        scratch_shapes=[pltpu.VMEM((tracks, one, channels), jnp.bfloat16)]
        + [pltpu.VMEM(first_norm_scale.shape, jnp.float32)] * 2
        + [pltpu.VMEM((channels, filters), jnp.bfloat16), pltpu.SemaphoreType.DMA((4,))],
        compiler_params=params,
        cost_estimate=cost(one, point=0),
    )(*far)
    inter_0 = cross(inter)
    local_0, intra = pl.pallas_call(
        functools.partial(entry_kernel, one),
        in_specs=[vmem] * 4,
        out_specs=[vmem] * 2,
        out_shape=[sums(rows), halo(one)],
        compiler_params=params,
        cost_estimate=cost(rows, point=0),
    )(tower_in, *norms, conv_weight)
    intra_0 = across(intra)

    edges, middle, inner, ends = (0, two), (two, three), (three, rows - two), (rows - two, rows)
    near = (three, rows)
    stream_1p, _, (local_1p,) = step(
        0, inner,
        [(everything, tower_in)],
        [(everything, False, local_0)],
        [],
        [((two, rows), [("here", inner, 0), ("out", inner, -two), ("inn", inner, two)])],
    )
    stream_1f, (inter,), (here_1f, inn_1f) = step(
        0, edges,
        [(everything, tower_in)],
        [(everything, False, local_0), ((0, one), True, inter_0)],
        [("out", edges)],
        [(edges, [("here", edges, 0)]), (middle, [("inn", edges, two)])],
        after=(local_1p,),
    )
    inter_1 = cross(inter)
    stream_1m, _, (local_1m,) = step(
        0, middle,
        [(everything, tower_in)],
        [(everything, False, local_0)],
        [],
        [((0, rows - two), [("here", middle, 0), ("out", middle, -two), ("inn", middle, two)])],
        after=(here_1f,),
    )
    stream_1e, (intra,), (local_1e,) = step(
        0, ends,
        [(everything, tower_in)],
        [(everything, False, local_0), ((rows - one, rows), False, intra_0)],
        [("inn", ends)],
        [((three, rows), [("here", ends, 0), ("out", ends, -two)])],
        after=(local_1m,),
    )
    intra_1 = across(intra)

    stream_2m, (inter,), _ = step(
        1, middle,
        [(middle, stream_1m)],
        [
            ((two, rows), False, local_1p),
            ((0, rows - two), False, local_1m),
            (middle, False, inn_1f),
        ],
        [("out", middle)],
        [],
        after=(local_1e,),
    )
    inter_2m = cross(inter)
    stream_2n, (intra,), (local_2n, here_2m, inn_2m) = step(
        1, near,
        [(inner, stream_1p), (ends, stream_1e)],
        [
            ((two, rows), False, local_1p),
            ((0, rows - two), False, local_1m),
            (near, False, local_1e),
            (ends, False, intra_1),
        ],
        [("inn", near)],
        [(everything, [("here", near, 0), ("out", near, -three)])],
        late=[
            (
                middle, stream_2m,
                [(middle, [("here", middle, 0)]), ((two + three, rows), [("inn", middle, three)])],
            )
        ],
    )
    intra_2 = across(intra)
    stream_2f, (inter,), (here_2f, inn_2f) = step(
        1, edges,
        [(edges, stream_1f)],
        [
            ((0, rows - two), False, local_1m),
            (edges, False, here_1f),
            (edges, True, inter_1),
        ],
        [("out", edges)],
        [(edges, [("here", edges, 0)]), ((three, three + two), [("inn", edges, three)])],
        after=(local_2n,),
    )
    inter_2f = cross(inter)

    stream_3n, (inter, intra), (local_3n,) = step(
        2, near,
        [(near, stream_2n)],
        [
            (everything, False, local_2n),
            ((three, three + two), False, inn_2f),
            ((two + three, rows), False, inn_2m),
            (near, False, intra_2),
        ],
        [("out", near), ("inn", near)],
        [(near, [("here", near, 0)])],
    )
    inter_3n, kept_3n = cross(inter), intra
    parts = [(0, tracks // 2), (tracks // 2, tracks - tracks // 2)]
    last, after = [], (local_3n,)
    for first, part in parts:
        stream_3f, (inter, intra), (local_3f,) = step(
            2, (0, three),
            [((0, two), stream_2f), (middle, stream_2m)],
            [
                (everything, False, local_2n),
                ((0, two), False, here_2f),
                (middle, False, here_2m),
                ((0, two), True, inter_2m),
                (middle, True, inter_2f),
            ],
            [("out", (0, three)), ("inn", (0, three))],
            [((0, three), [("here", (0, three), 0)])],
            after=after, first=first, part=part,
        )
        after = (local_3f,)
        if first == 0:
            kept_3n, intra = lax.optimization_barrier((kept_3n, intra))
            intra_3n = across(kept_3n)
        last.append((stream_3f, local_3f, cross(inter), across(intra)))

    far_ends, near_ends = [], []
    for (first, part), (stream_3f, local_3f, inter, intra) in zip(parts, last):
        far_ends.append(
            (first, part, (0, 0, first, first), (stream_3f, local_3f, intra_3n, inter_3n))
        )
        near_ends.append((first, part, (first, first, 0, 0), (stream_3n, local_3n, intra, inter)))
    out = []
    for q, chosen in [((0, three), far_ends)] + [(near, [end]) for end in near_ends]:
        count, total = q[1] - q[0], sum(part for _, part, _, _ in chosen)
        arrays = [array for *_, group in chosen for array in group]
        out = [
            pl.pallas_call(
                functools.partial(
                    last_kernel, blocks - 1, q, rows, [end[:3] for end in chosen]
                ),
                in_specs=[vmem] * (len(arrays) + 3) + [hbm] * len(out),
                out_specs=hbm,
                out_shape=jax.ShapeDtypeStruct(tower_in.shape, jnp.bfloat16),
                scratch_shapes=[
                    pltpu.VMEM((total, count, channels), jnp.bfloat16),
                    pltpu.SemaphoreType.DMA((total,)),
                ],
                input_output_aliases={len(arrays) + 3: 0} if out else {},
                compiler_params=params,
                cost_estimate=cost(count, conv=0, part=total),
            )(*arrays, *mids, *out)
        ]
    return out[0]


def solution(mesh):
    placed = (P("groups", "seq", None), P(), P(), P(), P(), P(), P())
    return jax.shard_map(
        local, mesh=mesh, in_specs=placed, out_specs=P("groups", "seq", None), check_vma=False
    )
```
